512 devices in a mesh: node: 128 (over y, z, core), rep: 4 (over x).
Axes of the slice: x: 4, y: 8, z: 8, core: 2. Of those that a mesh axis runs over, the one named last changes fastest.
Arguments:
- history_in: bfloat16 [262144, 128], P('node'), may hold values from 0 to 2
- history_mid: bfloat16 [262144, 128], P('node'), may hold values from 0 to 2
- current: bfloat16 [131072, 128], P(('node', 'rep')), may hold values from 0 to 2
- initial: bfloat16 [131072, 128], P(('node', 'rep')), may hold values from 0 to 2
- batch_rows: int32 [131072], P(('node', 'rep')), may hold values from 0 to 2047, as said below
- halo_rows: int32 [512, 128, 8], P(('node', 'rep')), may hold values from 0 to 2047
- halo_count: int32 [512, 128], P(('node', 'rep')), may hold values from 1 to 8, as said below
- adj_cols: int32 [512, 2, 8], P(('node', 'rep')), may hold values from 0 to 9, as said below
- adj_vals: bfloat16 [512, 2, 8, 128, 128], P(('node', 'rep')), may hold values from -0.1875 to 0.1875
- upstream: bfloat16 [131072, 128], P(('node', 'rep')), may hold values from -6 to 6
- weight_a: bfloat16 [128, 128], replicated, may hold values from -0.5 to 0.5
- weight_b: bfloat16 [128, 128], replicated, may hold values from -0.5 to 0.5
Outputs:
- final_out: bfloat16 [131072, 128], P(('node', 'rep'))
- history_in_new: bfloat16 [262144, 128], P('node')
- history_mid_new: bfloat16 [262144, 128], P('node')
- grad_a: float32 [128, 128], replicated
- grad_b: float32 [128, 128], replicated
The draws below stay inside these ranges and needn't reach their ends.
Inputs may be any that keep to these rules, and one draw needn't show every extreme that they name: `batch_rows`: for each index of node the 4 replicas' batch rows are distinct and cover half of the shard. `halo_count`: every count is at least 1; each device has an owner with all 8 slots live, and some owner has all 8 slots live from every device. `adj_cols`: each row block r names its own batch tile r among its 8 tiles; every halo tile is named by some row block.
All inputs are finite; a program needn't handle non-finite values.
Results may differ from the reference program's by a relative error of at most 0.011.
The reference program's roundings to bfloat16 on the way (of `support`, `gated_b`, `agg_grad` and `gated_a`) count: a program that leaves them out, or rounds other values in their place, can miss the bound.
Values may be sent and summed in bfloat16 or wider, within the bound.
A program may use at most 64 MiB of HBM per device.

```python
import math
import jax
import jax.numpy as jnp
from jax import lax

H = 128
TILE = 128
NB = 8
HALO_TILES = 8
RB = 2
BATCH = 256
SHARD = 2048
NODES = 262144
ROWS_ALL = 131072
CAP = 8
N_NODE = 128
N_REP = 4


def draw_halo_count(key, part):
    key = jax.random.fold_in(key, 1)
    devices = N_NODE * N_REP
    count_key, own_key, common_key = jax.random.split(key, 3)
    counts = jax.random.randint(count_key, (devices, N_NODE), 1, CAP + 1).astype(jnp.int32)
    full_owner = jax.random.randint(own_key, (devices,), 0, N_NODE).astype(jnp.int32)
    device_ids = jnp.arange(devices, dtype=jnp.int32)
    counts = counts.at[device_ids, full_owner].set(CAP)
    common_owner = jax.random.randint(common_key, (), 0, N_NODE).astype(jnp.int32)
    owner_ids = jnp.arange(N_NODE, dtype=jnp.int32)[None, :]
    counts = jnp.where(owner_ids == common_owner, CAP, counts)
    return counts.astype(jnp.int32)


def draw_adj_cols(key, part):
    key = jax.random.fold_in(key, 2)
    devices = N_NODE * N_REP
    block_ids = jnp.arange(RB, dtype=jnp.int32)[:, None]
    slot_ids = jnp.arange(NB - 2, dtype=jnp.int32)[None, :]
    halo_columns = RB + (block_ids * (NB - 2) + slot_ids) % HALO_TILES
    halo_columns = jnp.broadcast_to(halo_columns[None, :, :], (devices, RB, NB - 2))
    own_tile = jnp.broadcast_to(block_ids[None, :, :], (devices, RB, 1))
    next_tile = jnp.broadcast_to(((block_ids + 1) % RB)[None, :, :], (devices, RB, 1))
    columns = jnp.concatenate([own_tile, next_tile, halo_columns], -1).reshape(devices * RB, NB)
    block_keys = jax.random.split(key, devices * RB)

    def shuffle(single_key):
        return jax.random.permutation(single_key, NB)
    orders = jax.vmap(shuffle)(block_keys).astype(jnp.int32)
    return jnp.take_along_axis(columns, orders, axis=1).reshape(devices, RB, NB).astype(jnp.int32)


def draw_batch_rows(key, part):
    key = jax.random.fold_in(key, 3)
    node_keys = jax.random.split(key, N_NODE)

    def choose(single_key):
        return jax.random.permutation(single_key, SHARD)[:N_REP * BATCH]
    return jax.vmap(choose)(node_keys).reshape(-1).astype(jnp.int32)


def with_ends(values, key, low, top_value):
    longest = values.shape.index(max(values.shape))
    spots = []
    for shift in (0, 1):
        where = [jax.random.randint(jax.random.fold_in(key, axis), (), 0, length) for axis, length in enumerate(values.shape)]
        where[longest] = (where[longest] + shift) % values.shape[longest]
        spots.append(tuple(where))
    return values.at[spots[0]].set(low).at[spots[1]].set(top_value)


def levels(stream_key, extent, cuts, low, largest):
    gain, own = 1.0, jax.random.fold_in(stream_key, 6)
    for dim, parts in cuts:
        steps = jnp.exp(jax.random.uniform(jax.random.fold_in(own, dim), (parts,), jnp.float32, low / len(cuts), largest / len(cuts)))
        gain = gain * jnp.repeat(steps, extent[dim] // parts).reshape([-1 if axis == dim else 1 for axis in range(len(extent))])
    return gain


def gaussian(key, shape, spread, limit, cuts=(), kind=jnp.bfloat16):
    values = jax.random.normal(key, shape, jnp.float32) * spread
    if len(cuts) > 0:
        values = levels(key, shape, cuts, -0.22, 0.18) * values
    return jnp.clip(values, min=-limit, max=limit).astype(kind)


def setup_inputs(seed: int = 0) -> dict:
    key_list = jax.random.split(jax.random.key(seed), 13)
    history_in = jnp.clip(2.0 * jax.random.uniform(key_list[0], (NODES, H), jnp.float32) ** levels(key_list[0], (NODES, H), ((0, 128),), -0.2, 0.2), 0.0, 2.0).astype(jnp.bfloat16)
    history_mid = jnp.clip(2.0 * jax.random.uniform(key_list[1], (NODES, H), jnp.float32) ** levels(key_list[1], (NODES, H), ((0, 128),), -0.2, 0.2), 0.0, 2.0).astype(jnp.bfloat16)
    current = jnp.clip(2.0 * jax.random.uniform(key_list[2], (ROWS_ALL, H), jnp.float32) ** levels(key_list[2], (ROWS_ALL, H), ((0, 512),), -0.2, 0.2), 0.0, 2.0).astype(jnp.bfloat16)
    initial = jnp.clip(2.0 * jax.random.uniform(key_list[3], (ROWS_ALL, H), jnp.float32) ** levels(key_list[3], (ROWS_ALL, H), ((0, 512),), -0.2, 0.2), 0.0, 2.0).astype(jnp.bfloat16)
    batch_rows = draw_batch_rows(jax.random.fold_in(key_list[12], 71), 0)
    halo_rows = with_ends(jax.random.randint(key_list[5], (N_NODE * N_REP, N_NODE, CAP), 0, SHARD), jax.random.fold_in(key_list[5], 1), 0, SHARD - 1).astype(jnp.int32)
    halo_count = draw_halo_count(jax.random.fold_in(key_list[12], 71), 0)
    adj_cols = draw_adj_cols(jax.random.fold_in(key_list[12], 71), 0)
    adj_vals = gaussian(key_list[8], (N_NODE * N_REP, RB, NB, TILE, TILE), (NB * TILE) ** -0.5, 0.1875, ((0, 512),))
    upstream = gaussian(key_list[9], (ROWS_ALL, H), 1.0, 6.0, ((0, 512),))
    weight_a = gaussian(key_list[10], (H, H), H ** -0.5, 0.5)
    weight_b = gaussian(key_list[11], (H, H), H ** -0.5, 0.5)
    return {"history_in": history_in, "history_mid": history_mid, "current": current, "initial": initial, "batch_rows": batch_rows, "halo_rows": halo_rows, "halo_count": halo_count, "adj_cols": adj_cols, "adj_vals": adj_vals, "upstream": upstream, "weight_a": weight_a, "weight_b": weight_b}


alpha_mix = 0.1
beta_first = math.log(1.0 + 0.5 / 3.0)
beta_second = math.log(1.0 + 0.5 / 4.0)

def gcn_layer(feature_tiles, columns, edge_tiles, initial_rows, weight, beta_rate):
    picked = feature_tiles[columns]
    aggregate = jnp.einsum('rkij,rkjh->rih', edge_tiles.astype(jnp.float32), picked.astype(jnp.float32), precision=lax.Precision.HIGHEST)
    aggregate = aggregate.reshape(-1, aggregate.shape[-1])
    support = ((1.0 - alpha_mix) * aggregate + alpha_mix * initial_rows.astype(jnp.float32)).astype(jnp.bfloat16)
    preact = (1.0 - beta_rate) * support.astype(jnp.float32) + beta_rate * jnp.dot(support, weight, preferred_element_type=jnp.float32)
    return (support, preact, jnp.maximum(preact, 0.0).astype(jnp.bfloat16))

def reference(history_in, history_mid, current, initial, batch_rows, halo_rows, halo_count, adj_cols, adj_vals, upstream, weight_a, weight_b):
    devices = N_NODE * N_REP
    shard_in = history_in.reshape(N_NODE, SHARD, H)
    shard_mid = history_mid.reshape(N_NODE, SHARD, H)
    owner_ids = jnp.arange(N_NODE, dtype=jnp.int32)[:, None]

    def one_device(device_item):
        current_rows, initial_rows, owner_rows, counts, columns, edge_tiles, upstream_rows = device_item
        live_mask = (jnp.arange(CAP, dtype=jnp.int32)[None, :] < counts[:, None])[:, :, None]
        halo_a = jnp.where(live_mask, shard_in[owner_ids, owner_rows], 0).astype(jnp.bfloat16).reshape(HALO_TILES, TILE, H)
        halo_b = jnp.where(live_mask, shard_mid[owner_ids, owner_rows], 0).astype(jnp.bfloat16).reshape(HALO_TILES, TILE, H)
        tiles_a = jnp.concatenate([current_rows.reshape(RB, TILE, H), halo_a], 0)
        support_a, preact_a, fresh_a = gcn_layer(tiles_a, columns, edge_tiles, initial_rows, weight_a, beta_first)
        tiles_b = jnp.concatenate([fresh_a.reshape(RB, TILE, H), halo_b], 0)
        support_b, preact_b, final_rows = gcn_layer(tiles_b, columns, edge_tiles, initial_rows, weight_b, beta_second)
        gated_b = jnp.where(preact_b > 0, upstream_rows.astype(jnp.float32), 0.0).astype(jnp.bfloat16)
        part_b = beta_second * jnp.dot(support_b.T, gated_b, preferred_element_type=jnp.float32)
        support_grad = (1.0 - beta_second) * gated_b.astype(jnp.float32) + beta_second * jnp.dot(gated_b, weight_b.T, preferred_element_type=jnp.float32)
        agg_grad = ((1.0 - alpha_mix) * support_grad).astype(jnp.bfloat16)
        onehot = (columns[:, :, None] == jnp.arange(RB, dtype=jnp.int32)[None, None, :]).astype(jnp.float32)
        contrib = jnp.einsum('rkij,rih->rkjh', edge_tiles.astype(jnp.float32), agg_grad.reshape(RB, TILE, H).astype(jnp.float32), precision=lax.Precision.HIGHEST)
        fresh_grad = jnp.einsum('rkc,rkjh->cjh', onehot, contrib, precision=lax.Precision.HIGHEST).reshape(BATCH, H)
        gated_a = jnp.where(preact_a > 0, fresh_grad, 0.0).astype(jnp.bfloat16)
        part_a = beta_first * jnp.dot(support_a.T, gated_a, preferred_element_type=jnp.float32)
        return (final_rows, fresh_a, part_a, part_b)
    items = (current.reshape(devices, BATCH, H), initial.reshape(devices, BATCH, H), halo_rows, halo_count, adj_cols, adj_vals, upstream.reshape(devices, BATCH, H))
    final_rows, fresh_all, parts_a, parts_b = lax.map(one_device, items)
    scale = 1.0 / math.sqrt(ROWS_ALL)
    grad_a = lax.optimization_barrier(jnp.sum(parts_a, axis=0)) * scale
    grad_b = lax.optimization_barrier(jnp.sum(parts_b, axis=0)) * scale
    owned = batch_rows.reshape(N_NODE, N_REP * BATCH)
    history_in_new = shard_in.at[owner_ids, owned].set(current.reshape(N_NODE, N_REP * BATCH, H)).reshape(NODES, H)
    history_mid_new = shard_mid.at[owner_ids, owned].set(fresh_all.reshape(N_NODE, N_REP * BATCH, H)).reshape(NODES, H)
    return (final_rows.reshape(ROWS_ALL, H), history_in_new, history_mid_new, grad_a, grad_b)
```

```python
import functools
import math

import jax
import jax.numpy as jnp
from jax import lax
from jax.experimental import pallas as pl
from jax.experimental.pallas import tpu as pltpu
from jax.sharding import PartitionSpec as P

ALPHA = 0.1
BETA_A = math.log(1.0 + 0.5 / 3.0)
BETA_B = math.log(1.0 + 0.5 / 4.0)
MESH = pl.DeviceIdType.MESH
F32 = jnp.float32
BF16 = jnp.bfloat16

NY = 8
NW = 16
NX = 4
CAP = 8
TILE = 128
H = 128
BATCH = 256
SHARD = 2048
RB = 2
NB = 8
W_ORDER = (8, 7, 9, 6, 10, 5, 11, 4, 12, 3, 13, 2, 14, 1, 15, 0)
CHUNK = 4
ROWS = NY * CAP * CHUNK
PARTS = 8
BLOCK = SHARD // PARTS


def fill(ref, sem):
    pltpu.make_async_copy(ref, ref, sem).wait()


def dot(lhs, rhs):
    return jnp.dot(lhs, rhs, preferred_element_type=F32)


def dot_t(lhs, rhs):
    return lax.dot_general(lhs, rhs, (((0,), (0,)), ((), ())), preferred_element_type=F32)


def kernel(
    halo_rows,
    halo_count,
    batch_rows,
    cols,
    hist_in,
    hist_mid,
    current,
    initial,
    upstream,
    adj,
    weight_a,
    weight_b,
    final_out,
    new_in,
    new_mid,
    grad_a,
    grad_b,
    asked_y,
    asked_t,
    ask_row,
    asked_w,
    hist,
    onehot,
    rows_out,
    halo,
    tiles,
    adj_v,
    cur_all,
    fresh_all,
    br_all,
    refresh,
    base_mid,
    init_v,
    up_v,
    wa_v,
    wb_v,
    f_fwd,
    f_bwd,
    part,
    sum_w,
    sum_y,
    sum_x,
    total,
    load_sem,
    y_sem,
    w_sem,
    h_send,
    h_recv,
    rep_sem,
    red_sem,
    ready,
):
    node, x = lax.axis_index("node"), lax.axis_index("rep")
    y, w = node // NW, node % NW

    def dev(yy, ww, xx):
        return (yy * NW + ww, xx)

    def send(src, dst, s_sem, r_sem, device):
        pltpu.make_async_remote_copy(
            src_ref=src, dst_ref=dst, send_sem=s_sem, recv_sem=r_sem, device_id=device, device_id_type=MESH
        ).start()

    loads = [
        (hist_in, hist.at[:, pl.ds(0, H)]),
        (hist_mid, hist.at[:, pl.ds(H, H)]),
        (current, cur_all.at[x]),
        (adj, adj_v),
        (initial, init_v),
        (upstream, up_v),
        (weight_a, wa_v),
        (weight_b, wb_v),
    ]
    copies = [pltpu.make_async_copy(s, d, load_sem.at[i]) for i, (s, d) in enumerate(loads)]
    for c in copies:
        c.start()

    barrier = pltpu.get_barrier_semaphore()
    for k in range(1, NY):
        pl.semaphore_signal(barrier, inc=1, device_id=dev((y + k) % NY, w, x), device_id_type=MESH)
    for k in range(1, NW):
        pl.semaphore_signal(barrier, inc=1, device_id=dev(y, (w + k) % NW, x), device_id_type=MESH)
    for k in range(1, NX):
        pl.semaphore_signal(barrier, inc=1, device_id=dev(y, w, (x + k) % NX), device_id_type=MESH)

    slot = lax.broadcasted_iota(jnp.int32, (CAP, NY * NW), 0)
    asked_y[y] = jnp.where(slot < halo_count[...], halo_rows[...], -1)
    br_all[x] = batch_rows[...]
    pl.semaphore_wait(barrier, NY + NW + NX - 3)

    for k in range(1, NY):
        send(asked_y.at[y], asked_y.at[y], y_sem.at[0], y_sem.at[1], dev((y + k) % NY, w, x))
    fill(asked_y.at[pl.ds(0, NY - 1)], y_sem.at[1])
    lists = asked_y[...].reshape(NY * CAP, NY * NW)
    lists = jnp.concatenate([lists, jnp.zeros((128 - NY * CAP, NY * NW), jnp.int32)], 0)
    asked_t[...] = lists.T
    mine = asked_t[pl.ds(pl.multiple_of(y * NW, NW), NW), :]
    for i in range(NW):
        ask_row[i] = mine[i : i + 1, :]
    for i, k in enumerate(W_ORDER):
        if k:
            to = (w + k) % NW
            send(ask_row.at[to], asked_w.at[i], w_sem.at[0], w_sem.at[1], dev(y, to, x))
    asked_w[NW - 1] = ask_row[w]

    copies[2].wait()
    for k in range(1, NX):
        to = dev(y, w, (x + k) % NX)
        send(br_all.at[x], br_all.at[x], rep_sem.at[0], rep_sem.at[1], to)
        send(cur_all.at[x], cur_all.at[x], rep_sem.at[2], rep_sem.at[3], to)

    fill(asked_w.at[pl.ds(0, NW - 1)], w_sem.at[1])
    wanted = jnp.concatenate([asked_w[i] for i in range(NW)] + [jnp.zeros((128 - NW, 128), jnp.int32)], 0)
    asked_t[...] = wanted.T
    wanted = asked_t[pl.ds(0, NY * CAP), :]
    lane = lax.broadcasted_iota(jnp.int32, (NY * CAP, SHARD), 1)
    for c in range(NW // CHUNK):
        for q in range(CHUNK):
            i = c * CHUNK + q
            hit = jnp.broadcast_to(wanted[:, i : i + 1], (NY * CAP, SHARD)) == lane
            onehot[pl.ds(q * NY * CAP, NY * CAP), :] = hit.astype(F32).astype(BF16)
        if c == 0:
            copies[0].wait()
            copies[1].wait()
        got = dot(onehot[...], hist[...])
        both = jnp.concatenate(
            [got[:, :H].reshape(CHUNK * NY, CAP, H), got[:, H:].reshape(CHUNK * NY, CAP, H)], 1
        )
        rows_out[pl.ds(c * CHUNK, CHUNK)] = both.astype(BF16).reshape(CHUNK, NY, 2 * CAP, H)
        for q in range(CHUNK):
            i = c * CHUNK + q
            k = W_ORDER[i]
            to_w = (w + NW - k) % NW

            def reply(ky, carry, i=i, to_w=to_w):
                to_y = (y + ky) % NY
                send(rows_out.at[i, to_y], halo.at[y, w], h_send, h_recv.at[y], dev(to_y, to_w, x))
                return carry

            lax.fori_loop(0 if k else 1, NY, reply, 0)
    halo[y, w] = rows_out[NW - 1, y]

    copies[3].wait()
    for r in range(RB):
        for c in range(RB):
            acc = jnp.zeros((TILE, TILE), F32)
            for k in range(NB):
                acc = acc + jnp.where(cols[r, k] == c, adj_v[r, k].astype(F32), 0.0)
            high = acc.astype(BF16)
            low = (acc - high.astype(F32)).astype(BF16)
            rs, cs = pl.ds(r * TILE, TILE), pl.ds(c * TILE, TILE)
            f_fwd[rs, cs] = high
            f_fwd[rs, pl.ds(BATCH + c * TILE, TILE)] = low
            acc_t = acc.T
            high_t = acc_t.astype(BF16)
            f_bwd[cs, rs] = high_t
            f_bwd[cs, pl.ds(BATCH + r * TILE, TILE)] = (acc_t - high_t.astype(F32)).astype(BF16)
    for c in range(RB):
        tiles[c, :, pl.ds(0, H)] = cur_all[x, pl.ds(c * TILE, TILE), :]
        tiles[c, :, pl.ds(H, H)] = jnp.zeros((TILE, H), BF16)

    fill(br_all.at[pl.ds(0, NX - 1)], rep_sem.at[1])
    fill(cur_all.at[pl.ds(0, NX - 1)], rep_sem.at[3])
    for p in range(PARTS):
        rows = pl.ds(p * BLOCK, BLOCK)
        row = p * BLOCK + lax.broadcasted_iota(jnp.int32, (BLOCK, BATCH), 0)
        for r in range(NX):
            refresh[rows, pl.ds(r * BATCH, BATCH)] = (br_all[r] == row).astype(F32).astype(BF16)
    new_rows = jnp.concatenate([cur_all[...].reshape(NX * BATCH, H), jnp.ones((NX * BATCH, H), BF16)], 1)
    for p in range(PARTS):
        rows = pl.ds(p * BLOCK, BLOCK)
        put = dot(refresh[rows, :], new_rows)
        kept = put[:, H:] == 0.0
        new_in[rows, :] = jnp.where(kept, hist[rows, pl.ds(0, H)].astype(F32), put[:, :H]).astype(BF16)
        base_mid[rows, :] = jnp.where(kept, hist[rows, pl.ds(H, H)].astype(F32), 0.0).astype(BF16)
    for c in copies[4:]:
        c.wait()

    for k in range(NY):
        yy = (y + k) % NY
        if k:
            fill(halo.at[yy], h_recv.at[yy])
        else:
            fill(halo.at[y, pl.ds(0, NW - 1)], h_recv.at[y])
        block = halo[yy].astype(F32)
        pair = [block[:, :CAP, :].reshape(TILE, H), block[:, CAP:, :].reshape(TILE, H)]
        tiles[RB + yy] = jnp.concatenate(pair, 1).astype(BF16)
    for k in range(1, NX):
        pl.semaphore_signal(ready, inc=1, device_id=dev(y, w, (x + k) % NX), device_id_type=MESH)

    sums = []
    for r in range(RB):
        left = jnp.concatenate([adj_v[r, k] for k in range(NB)], 1)
        right = jnp.concatenate([tiles[cols[r, k]] for k in range(NB)], 0)
        sums.append(dot(left, right))
    agg = jnp.concatenate(sums, 0)
    init = ALPHA * init_v[...].astype(F32)
    support_a = ((1.0 - ALPHA) * agg[:, :H] + init).astype(BF16)
    preact_a = (1.0 - BETA_A) * support_a.astype(F32) + BETA_A * dot(support_a, wa_v[...])
    fresh = jnp.maximum(preact_a, 0.0).astype(BF16)
    fresh_all[x] = fresh
    for k in range(1, NX):
        send(fresh_all.at[x], fresh_all.at[x], rep_sem.at[4], rep_sem.at[5], dev(y, w, (x + k) % NX))
    agg_b = agg[:, H:] + dot(f_fwd[...], jnp.concatenate([fresh, fresh], 0))
    support_b = ((1.0 - ALPHA) * agg_b + init).astype(BF16)
    preact_b = (1.0 - BETA_B) * support_b.astype(F32) + BETA_B * dot(support_b, wb_v[...])
    final_out[...] = jnp.maximum(preact_b, 0.0).astype(BF16)
    gated_b = jnp.where(preact_b > 0, up_v[...].astype(F32), 0.0).astype(BF16)
    part[pl.ds(H, H), :] = BETA_B * dot_t(support_b, gated_b)
    back = lax.dot_general(gated_b, wb_v[...], (((1,), (1,)), ((), ())), preferred_element_type=F32)
    support_grad = (1.0 - BETA_B) * gated_b.astype(F32) + BETA_B * back
    agg_grad = ((1.0 - ALPHA) * support_grad).astype(BF16)
    fresh_grad = dot(f_bwd[...], jnp.concatenate([agg_grad, agg_grad], 0))
    gated_a = jnp.where(preact_a > 0, fresh_grad, 0.0).astype(BF16)
    part[pl.ds(0, H), :] = BETA_A * dot_t(support_a, gated_a)

    piece = 2 * H // NW
    for k in W_ORDER[:-1]:
        to = (w + k) % NW
        rows = pl.ds(pl.multiple_of(to * piece, piece), piece)
        send(part.at[rows, :], sum_w.at[w], red_sem.at[0], red_sem.at[1], dev(y, to, x))
    sum_w[w] = part[pl.ds(pl.multiple_of(w * piece, piece), piece), :]
    fill(sum_w.at[pl.ds(0, NW - 1)], red_sem.at[1])
    sum_y[y] = jnp.sum(sum_w[...], 0)
    for k in range(1, NY):
        send(sum_y.at[y], sum_y.at[y], red_sem.at[2], red_sem.at[3], dev((y + k) % NY, w, x))
    fill(sum_y.at[pl.ds(0, NY - 1)], red_sem.at[3])
    sum_x[x] = jnp.sum(sum_y[...], 0)
    for k in range(1, NX):
        send(sum_x.at[x], sum_x.at[x], red_sem.at[4], red_sem.at[5], dev(y, w, (x + k) % NX))
    fill(sum_x.at[pl.ds(0, NX - 1)], red_sem.at[5])
    total[w] = jnp.sum(sum_x[...], 0) * (1.0 / math.sqrt(NY * NW * NX * BATCH))
    for k in W_ORDER[:-1]:
        send(total.at[w], total.at[w], red_sem.at[6], red_sem.at[7], dev(y, (w + k) % NW, x))

    pl.semaphore_wait(ready, NX - 1)
    fill(fresh_all.at[pl.ds(0, NX - 1)], rep_sem.at[5])
    fresh_rows = fresh_all[...].reshape(NX * BATCH, H)
    for p in range(PARTS):
        rows = pl.ds(p * BLOCK, BLOCK)
        put = dot(refresh[rows, :], fresh_rows)
        new_mid[rows, :] = (put + base_mid[rows, :].astype(F32)).astype(BF16)

    fill(total.at[pl.ds(0, NW - 1)], red_sem.at[7])
    half = NW // 2
    grad_a[...] = total[pl.ds(0, half)].reshape(H, H)
    grad_b[...] = total[pl.ds(half, half)].reshape(H, H)

    fill(asked_y.at[pl.ds(0, NY - 1)], y_sem.at[0])
    fill(asked_w.at[pl.ds(0, NW - 1)], w_sem.at[0])
    fill(br_all.at[pl.ds(0, NX - 1)], rep_sem.at[0])
    fill(cur_all.at[pl.ds(0, NX - 1)], rep_sem.at[2])
    fill(fresh_all.at[pl.ds(0, NX - 1)], rep_sem.at[4])
    for k in range(NY):
        fill(halo.at[k] if k else halo.at[k, pl.ds(0, NW - 1)], h_send)
    fill(sum_w.at[pl.ds(0, NW - 1)], red_sem.at[0])
    fill(sum_y.at[pl.ds(0, NY - 1)], red_sem.at[2])
    fill(sum_x.at[pl.ds(0, NX - 1)], red_sem.at[4])
    fill(total.at[pl.ds(0, NW - 1)], red_sem.at[6])


def on_device(
    history_in,
    history_mid,
    current,
    initial,
    batch_rows,
    halo_rows,
    halo_count,
    adj_cols,
    adj_vals,
    upstream,
    weight_a,
    weight_b,
):
    vmem = pl.BlockSpec(memory_space=pltpu.VMEM)
    smem = pl.BlockSpec(memory_space=pltpu.SMEM)
    hbm = pl.BlockSpec(memory_space=pltpu.HBM)
    sds = jax.ShapeDtypeStruct
    dma = pltpu.SemaphoreType.DMA
    piece = 2 * H // NW
    return pl.pallas_call(
        kernel,
        name="gcn",
        out_shape=(
            sds((BATCH, H), BF16),
            sds((SHARD, H), BF16),
            sds((SHARD, H), BF16),
            sds((H, H), F32),
            sds((H, H), F32),
        ),
        in_specs=[vmem, vmem, vmem, smem] + [hbm] * 8,
        out_specs=(vmem,) * 5,
        scratch_shapes=[
            pltpu.VMEM((NY, CAP, NY * NW), jnp.int32),
            pltpu.VMEM((128, 128), jnp.int32),
            pltpu.VMEM((NW, 1, 128), jnp.int32),
            pltpu.VMEM((NW, 1, 128), jnp.int32),
            pltpu.VMEM((SHARD, 2 * H), BF16),
            pltpu.VMEM((ROWS, SHARD), BF16),
            pltpu.VMEM((NW, NY, 2 * CAP, H), BF16),
            pltpu.VMEM((NY, NW, 2 * CAP, H), BF16),
            pltpu.VMEM((RB + NY, TILE, 2 * H), BF16),
            pltpu.VMEM((RB, NB, TILE, TILE), BF16),
            pltpu.VMEM((NX, BATCH, H), BF16),
            pltpu.VMEM((NX, BATCH, H), BF16),
            pltpu.VMEM((NX, 1, BATCH), jnp.int32),
            pltpu.VMEM((SHARD, NX * BATCH), BF16),
            pltpu.VMEM((SHARD, H), BF16),
            pltpu.VMEM((BATCH, H), BF16),
            pltpu.VMEM((BATCH, H), BF16),
            pltpu.VMEM((H, H), BF16),
            pltpu.VMEM((H, H), BF16),
            pltpu.VMEM((BATCH, 2 * BATCH), BF16),
            pltpu.VMEM((BATCH, 2 * BATCH), BF16),
            pltpu.VMEM((2 * H, H), F32),
            pltpu.VMEM((NW, piece, H), F32),
            pltpu.VMEM((NY, piece, H), F32),
            pltpu.VMEM((NX, piece, H), F32),
            pltpu.VMEM((NW, piece, H), F32),
            dma((8,)),
            dma((2,)),
            dma((2,)),
            dma,
            dma((NY,)),
            dma((6,)),
            dma((8,)),
            pltpu.SemaphoreType.REGULAR,
        ],
        compiler_params=pltpu.CompilerParams(
            collective_id=0, has_side_effects=True, vmem_limit_bytes=40 * 2**20
        ),
    )(
        halo_rows[0].T,
        halo_count,
        batch_rows[None, :],
        adj_cols[0],
        history_in,
        history_mid,
        current,
        initial,
        upstream,
        adj_vals[0],
        weight_a,
        weight_b,
    )


def solution(mesh):
    both = ("node", "rep")
    in_specs = (
        P("node", None),
        P("node", None),
        P(both, None),
        P(both, None),
        P(both),
        P(both, None, None),
        P(both, None),
        P(both, None, None),
        P(both, None, None, None, None),
        P(both, None),
        P(),
        P(),
    )
    out_specs = (P(both, None), P("node", None), P("node", None), P(), P())
    return jax.shard_map(on_device, mesh=mesh, in_specs=in_specs, out_specs=out_specs, check_vma=False)
```

```python
import functools
import math

import jax
import jax.numpy as jnp
from jax import lax
from jax.experimental import pallas as pl
from jax.experimental.pallas import tpu as pltpu
from jax.sharding import PartitionSpec as P

ALPHA = 0.1
BETA_A = math.log(1.0 + 0.5 / 3.0)
BETA_B = math.log(1.0 + 0.5 / 4.0)
MESH = pl.DeviceIdType.MESH
F32 = jnp.float32
BF16 = jnp.bfloat16

NY = 8
NW = 16
NX = 4
CAP = 8
TILE = 128
H = 128
BATCH = 256
SHARD = 2048
RB = 2
NB = 8
W_ORDER = (8, 7, 9, 6, 10, 5, 11, 4, 12, 3, 13, 2, 14, 1, 15, 0)
CHUNK = 4
ROWS = NY * CAP * CHUNK
PARTS = 8
BLOCK = SHARD // PARTS
VMEM = 40 * 2**20


def fill(ref, sem):
    pltpu.make_async_copy(ref, ref, sem).wait()


def dot(lhs, rhs):
    return jnp.dot(lhs, rhs, preferred_element_type=F32)


def dot_t(lhs, rhs):
    return lax.dot_general(lhs, rhs, (((0,), (0,)), ((), ())), preferred_element_type=F32)


def kernel(
    halo_rows,
    halo_count,
    batch_rows,
    adj_cols,
    hist_in,
    hist_mid,
    current,
    initial,
    upstream,
    adj,
    weight_a,
    weight_b,
    final_out,
    new_in,
    new_mid,
    grad_a,
    grad_b,
    list_v,
    count_v,
    cols,
    asked_y,
    asked_t,
    ask_row,
    asked_w,
    hist,
    onehot,
    rows_out,
    halo,
    tiles,
    adj_v,
    cur_all,
    fresh_all,
    br_all,
    refresh,
    base_mid,
    init_v,
    up_v,
    wa_v,
    wb_v,
    f_fwd,
    f_bwd,
    part,
    sum_w,
    sum_y,
    sum_x,
    total,
    load_sem,
    y_sem,
    w_sem,
    h_send,
    h_recv,
    rep_sem,
    red_sem,
    ready,
):
    node, x = lax.axis_index("node"), lax.axis_index("rep")
    y, w = node // NW, node % NW

    def dev(yy, ww, xx):
        return (yy * NW + ww, xx)

    def send(src, dst, s_sem, r_sem, device):
        pltpu.make_async_remote_copy(
            src_ref=src, dst_ref=dst, send_sem=s_sem, recv_sem=r_sem, device_id=device, device_id_type=MESH
        ).start()

    loads = [
        (halo_rows, list_v),
        (halo_count, count_v),
        (batch_rows, br_all.at[x]),
        (adj_cols, cols),
        (hist_in, hist.at[:, pl.ds(0, H)]),
        (hist_mid, hist.at[:, pl.ds(H, H)]),
        (current, cur_all.at[x]),
        (adj, adj_v),
        (initial, init_v),
        (upstream, up_v),
        (weight_a, wa_v),
        (weight_b, wb_v),
    ]
    copies = [pltpu.make_async_copy(s, d, load_sem.at[i]) for i, (s, d) in enumerate(loads)]
    for c in copies:
        c.start()

    barrier = pltpu.get_barrier_semaphore()
    for k in range(1, NY):
        pl.semaphore_signal(barrier, inc=1, device_id=dev((y + k) % NY, w, x), device_id_type=MESH)
    for k in range(1, NW):
        pl.semaphore_signal(barrier, inc=1, device_id=dev(y, (w + k) % NW, x), device_id_type=MESH)
    for k in range(1, NX):
        pl.semaphore_signal(barrier, inc=1, device_id=dev(y, w, (x + k) % NX), device_id_type=MESH)

    slot = lax.broadcasted_iota(jnp.int32, (CAP, NY * NW), 0)
    copies[0].wait()
    copies[1].wait()
    asked_y[y] = jnp.where(slot < count_v[...], list_v[...], -1)
    pl.semaphore_wait(barrier, NY + NW + NX - 3)

    for k in range(1, NY):
        send(asked_y.at[y], asked_y.at[y], y_sem.at[0], y_sem.at[1], dev((y + k) % NY, w, x))
    fill(asked_y.at[pl.ds(0, NY - 1)], y_sem.at[1])
    lists = asked_y[...].reshape(NY * CAP, NY * NW)
    lists = jnp.concatenate([lists, jnp.zeros((128 - NY * CAP, NY * NW), jnp.int32)], 0)
    asked_t[...] = lists.T
    mine = asked_t[pl.ds(pl.multiple_of(y * NW, NW), NW), :]
    for i in range(NW):
        ask_row[i] = mine[i : i + 1, :]
    for i, k in enumerate(W_ORDER):
        if k:
            to = (w + k) % NW
            send(ask_row.at[to], asked_w.at[i], w_sem.at[0], w_sem.at[1], dev(y, to, x))
    asked_w[NW - 1] = ask_row[w]

    copies[2].wait()
    copies[6].wait()
    for k in range(1, NX):
        to = dev(y, w, (x + k) % NX)
        send(br_all.at[x], br_all.at[x], rep_sem.at[0], rep_sem.at[1], to)
        send(cur_all.at[x], cur_all.at[x], rep_sem.at[2], rep_sem.at[3], to)

    fill(asked_w.at[pl.ds(0, NW - 1)], w_sem.at[1])
    wanted = jnp.concatenate([asked_w[i] for i in range(NW)] + [jnp.zeros((128 - NW, 128), jnp.int32)], 0)
    asked_t[...] = wanted.T
    wanted = asked_t[pl.ds(0, NY * CAP), :]
    lane = lax.broadcasted_iota(jnp.int32, (NY * CAP, SHARD), 1)
    for c in range(NW // CHUNK):
        for q in range(CHUNK):
            i = c * CHUNK + q
            hit = jnp.broadcast_to(wanted[:, i : i + 1], (NY * CAP, SHARD)) == lane
            onehot[pl.ds(q * NY * CAP, NY * CAP), :] = hit.astype(F32).astype(BF16)
        if c == 0:
            copies[4].wait()
            copies[5].wait()
        got = dot(onehot[...], hist[...])
        both = jnp.concatenate(
            [got[:, :H].reshape(CHUNK * NY, CAP, H), got[:, H:].reshape(CHUNK * NY, CAP, H)], 1
        )
        rows_out[pl.ds(c * CHUNK, CHUNK)] = both.astype(BF16).reshape(CHUNK, NY, 2 * CAP, H)
        for q in range(CHUNK):
            i = c * CHUNK + q
            k = W_ORDER[i]
            to_w = (w + NW - k) % NW

            def reply(ky, carry, i=i, to_w=to_w):
                to_y = (y + ky) % NY
                send(rows_out.at[i, to_y], halo.at[y, w], h_send, h_recv.at[y], dev(to_y, to_w, x))
                return carry

            lax.fori_loop(0 if k else 1, NY, reply, 0)
    halo[y, w] = rows_out[NW - 1, y]

    copies[3].wait()
    copies[7].wait()
    for r in range(RB):
        for c in range(RB):
            acc = jnp.zeros((TILE, TILE), F32)
            for k in range(NB):
                acc = acc + jnp.where(cols[r, k] == c, adj_v[r, k].astype(F32), 0.0)
            high = acc.astype(BF16)
            low = (acc - high.astype(F32)).astype(BF16)
            rs, cs = pl.ds(r * TILE, TILE), pl.ds(c * TILE, TILE)
            f_fwd[rs, cs] = high
            f_fwd[rs, pl.ds(BATCH + c * TILE, TILE)] = low
            acc_t = acc.T
            high_t = acc_t.astype(BF16)
            f_bwd[cs, rs] = high_t
            f_bwd[cs, pl.ds(BATCH + r * TILE, TILE)] = (acc_t - high_t.astype(F32)).astype(BF16)
    for c in range(RB):
        tiles[c, :, pl.ds(0, H)] = cur_all[x, pl.ds(c * TILE, TILE), :]
        tiles[c, :, pl.ds(H, H)] = jnp.zeros((TILE, H), BF16)

    fill(br_all.at[pl.ds(0, NX - 1)], rep_sem.at[1])
    fill(cur_all.at[pl.ds(0, NX - 1)], rep_sem.at[3])
    for p in range(PARTS):
        rows = pl.ds(p * BLOCK, BLOCK)
        row = p * BLOCK + lax.broadcasted_iota(jnp.int32, (BLOCK, BATCH), 0)
        for r in range(NX):
            refresh[rows, pl.ds(r * BATCH, BATCH)] = (br_all[r] == row).astype(F32).astype(BF16)
    new_rows = jnp.concatenate([cur_all[...].reshape(NX * BATCH, H), jnp.ones((NX * BATCH, H), BF16)], 1)
    for p in range(PARTS):
        rows = pl.ds(p * BLOCK, BLOCK)
        put = dot(refresh[rows, :], new_rows)
        kept = put[:, H:] == 0.0
        new_in[rows, :] = jnp.where(kept, hist[rows, pl.ds(0, H)].astype(F32), put[:, :H]).astype(BF16)
        base_mid[rows, :] = jnp.where(kept, hist[rows, pl.ds(H, H)].astype(F32), 0.0).astype(BF16)
    for c in copies[8:]:
        c.wait()

    for k in range(NY):
        yy = (y + k) % NY
        if k:
            fill(halo.at[yy], h_recv.at[yy])
        else:
            fill(halo.at[y, pl.ds(0, NW - 1)], h_recv.at[y])
        block = halo[yy].astype(F32)
        pair = [block[:, :CAP, :].reshape(TILE, H), block[:, CAP:, :].reshape(TILE, H)]
        tiles[RB + yy] = jnp.concatenate(pair, 1).astype(BF16)
    for k in range(1, NX):
        pl.semaphore_signal(ready, inc=1, device_id=dev(y, w, (x + k) % NX), device_id_type=MESH)

    sums = []
    for r in range(RB):
        left = jnp.concatenate([adj_v[r, k] for k in range(NB)], 1)
        right = jnp.concatenate([tiles[cols[r, k]] for k in range(NB)], 0)
        sums.append(dot(left, right))
    agg = jnp.concatenate(sums, 0)
    init = ALPHA * init_v[...].astype(F32)
    support_a = ((1.0 - ALPHA) * agg[:, :H] + init).astype(BF16)
    preact_a = (1.0 - BETA_A) * support_a.astype(F32) + BETA_A * dot(support_a, wa_v[...])
    fresh = jnp.maximum(preact_a, 0.0).astype(BF16)
    fresh_all[x] = fresh
    for k in range(1, NX):
        send(fresh_all.at[x], fresh_all.at[x], rep_sem.at[4], rep_sem.at[5], dev(y, w, (x + k) % NX))
    agg_b = agg[:, H:] + dot(f_fwd[...], jnp.concatenate([fresh, fresh], 0))
    support_b = ((1.0 - ALPHA) * agg_b + init).astype(BF16)
    preact_b = (1.0 - BETA_B) * support_b.astype(F32) + BETA_B * dot(support_b, wb_v[...])
    final_out[...] = jnp.maximum(preact_b, 0.0).astype(BF16)
    gated_b = jnp.where(preact_b > 0, up_v[...].astype(F32), 0.0).astype(BF16)
    part[pl.ds(H, H), :] = BETA_B * dot_t(support_b, gated_b)
    back = lax.dot_general(gated_b, wb_v[...], (((1,), (1,)), ((), ())), preferred_element_type=F32)
    support_grad = (1.0 - BETA_B) * gated_b.astype(F32) + BETA_B * back
    agg_grad = ((1.0 - ALPHA) * support_grad).astype(BF16)
    fresh_grad = dot(f_bwd[...], jnp.concatenate([agg_grad, agg_grad], 0))
    gated_a = jnp.where(preact_a > 0, fresh_grad, 0.0).astype(BF16)
    part[pl.ds(0, H), :] = BETA_A * dot_t(support_a, gated_a)

    piece = 2 * H // NW
    for k in W_ORDER[:-1]:
        to = (w + k) % NW
        rows = pl.ds(pl.multiple_of(to * piece, piece), piece)
        send(part.at[rows, :], sum_w.at[w], red_sem.at[0], red_sem.at[1], dev(y, to, x))
    sum_w[w] = part[pl.ds(pl.multiple_of(w * piece, piece), piece), :]
    fill(sum_w.at[pl.ds(0, NW - 1)], red_sem.at[1])
    sum_y[y] = jnp.sum(sum_w[...], 0)
    for k in range(1, NY):
        send(sum_y.at[y], sum_y.at[y], red_sem.at[2], red_sem.at[3], dev((y + k) % NY, w, x))
    fill(sum_y.at[pl.ds(0, NY - 1)], red_sem.at[3])
    sum_x[x] = jnp.sum(sum_y[...], 0)
    for k in range(1, NX):
        send(sum_x.at[x], sum_x.at[x], red_sem.at[4], red_sem.at[5], dev(y, w, (x + k) % NX))
    fill(sum_x.at[pl.ds(0, NX - 1)], red_sem.at[5])
    total[w] = jnp.sum(sum_x[...], 0) * (1.0 / math.sqrt(NY * NW * NX * BATCH))
    for k in W_ORDER[:-1]:
        send(total.at[w], total.at[w], red_sem.at[6], red_sem.at[7], dev(y, (w + k) % NW, x))

    pl.semaphore_wait(ready, NX - 1)
    fill(fresh_all.at[pl.ds(0, NX - 1)], rep_sem.at[5])
    fresh_rows = fresh_all[...].reshape(NX * BATCH, H)
    for p in range(PARTS):
        rows = pl.ds(p * BLOCK, BLOCK)
        put = dot(refresh[rows, :], fresh_rows)
        new_mid[rows, :] = (put + base_mid[rows, :].astype(F32)).astype(BF16)

    fill(total.at[pl.ds(0, NW - 1)], red_sem.at[7])
    half = NW // 2
    grad_a[...] = total[pl.ds(0, half)].reshape(H, H)
    grad_b[...] = total[pl.ds(half, half)].reshape(H, H)

    fill(asked_y.at[pl.ds(0, NY - 1)], y_sem.at[0])
    fill(asked_w.at[pl.ds(0, NW - 1)], w_sem.at[0])
    fill(br_all.at[pl.ds(0, NX - 1)], rep_sem.at[0])
    fill(cur_all.at[pl.ds(0, NX - 1)], rep_sem.at[2])
    fill(fresh_all.at[pl.ds(0, NX - 1)], rep_sem.at[4])
    for k in range(NY):
        fill(halo.at[k] if k else halo.at[k, pl.ds(0, NW - 1)], h_send)
    fill(sum_w.at[pl.ds(0, NW - 1)], red_sem.at[0])
    fill(sum_y.at[pl.ds(0, NY - 1)], red_sem.at[2])
    fill(sum_x.at[pl.ds(0, NX - 1)], red_sem.at[4])
    fill(total.at[pl.ds(0, NW - 1)], red_sem.at[6])


def write_out(*refs):
    sems = refs[-1]
    copies = [pltpu.make_async_copy(refs[i], refs[5 + i], sems.at[i]) for i in range(5)]
    for c in copies:
        c.start()
    for c in copies:
        c.wait()


def on_device(
    history_in,
    history_mid,
    current,
    initial,
    batch_rows,
    halo_rows,
    halo_count,
    adj_cols,
    adj_vals,
    upstream,
    weight_a,
    weight_b,
):
    vmem = pl.BlockSpec(memory_space=pltpu.VMEM)
    hbm = pl.BlockSpec(memory_space=pltpu.HBM)
    sds = jax.ShapeDtypeStruct
    dma = pltpu.SemaphoreType.DMA
    piece = 2 * H // NW
    results = pl.pallas_call(
        kernel,
        name="gcn",
        out_shape=(
            sds((BATCH, H), BF16),
            sds((SHARD, H), BF16),
            sds((SHARD, H), BF16),
            sds((H, H), F32),
            sds((H, H), F32),
        ),
        in_specs=[hbm] * 12,
        out_specs=(vmem,) * 5,
        scratch_shapes=[
            pltpu.VMEM((CAP, NY * NW), jnp.int32),
            pltpu.VMEM((1, NY * NW), jnp.int32),
            pltpu.SMEM((RB, NB), jnp.int32),
            pltpu.VMEM((NY, CAP, NY * NW), jnp.int32),
            pltpu.VMEM((128, 128), jnp.int32),
            pltpu.VMEM((NW, 1, 128), jnp.int32),
            pltpu.VMEM((NW, 1, 128), jnp.int32),
            pltpu.VMEM((SHARD, 2 * H), BF16),
            pltpu.VMEM((ROWS, SHARD), BF16),
            pltpu.VMEM((NW, NY, 2 * CAP, H), BF16),
            pltpu.VMEM((NY, NW, 2 * CAP, H), BF16),
            pltpu.VMEM((RB + NY, TILE, 2 * H), BF16),
            pltpu.VMEM((RB, NB, TILE, TILE), BF16),
            pltpu.VMEM((NX, BATCH, H), BF16),
            pltpu.VMEM((NX, BATCH, H), BF16),
            pltpu.VMEM((NX, 1, BATCH), jnp.int32),
            pltpu.VMEM((SHARD, NX * BATCH), BF16),
            pltpu.VMEM((SHARD, H), BF16),
            pltpu.VMEM((BATCH, H), BF16),
            pltpu.VMEM((BATCH, H), BF16),
            pltpu.VMEM((H, H), BF16),
            pltpu.VMEM((H, H), BF16),
            pltpu.VMEM((BATCH, 2 * BATCH), BF16),
            pltpu.VMEM((BATCH, 2 * BATCH), BF16),
            pltpu.VMEM((2 * H, H), F32),
            pltpu.VMEM((NW, piece, H), F32),
            pltpu.VMEM((NY, piece, H), F32),
            pltpu.VMEM((NX, piece, H), F32),
            pltpu.VMEM((NW, piece, H), F32),
            dma((12,)),
            dma((2,)),
            dma((2,)),
            dma,
            dma((NY,)),
            dma((6,)),
            dma((8,)),
            pltpu.SemaphoreType.REGULAR,
        ],
        compiler_params=pltpu.CompilerParams(
            collective_id=0, has_side_effects=True, vmem_limit_bytes=VMEM
        ),
    )(*[pltpu.with_memory_space_constraint(a, pltpu.HBM) for a in (
        halo_rows[0].T,
        halo_count,
        batch_rows[None, :],
        adj_cols[0],
        history_in,
        history_mid,
        current,
        initial,
        upstream,
        adj_vals[0],
        weight_a,
        weight_b,
    )])
    return pl.pallas_call(
        write_out,
        name="write_out",
        out_shape=tuple(sds(r.shape, r.dtype) for r in results),
        in_specs=[vmem] * 5,
        out_specs=(hbm,) * 5,
        scratch_shapes=[dma((5,))],
        compiler_params=pltpu.CompilerParams(vmem_limit_bytes=4 * 2**20),
    )(*results)


def solution(mesh):
    both = ("node", "rep")
    in_specs = (
        P("node", None),
        P("node", None),
        P(both, None),
        P(both, None),
        P(both),
        P(both, None, None),
        P(both, None),
        P(both, None, None),
        P(both, None, None, None, None),
        P(both, None),
        P(),
        P(),
    )
    out_specs = (P(both, None), P("node", None), P("node", None), P(), P())
    return jax.shard_map(on_device, mesh=mesh, in_specs=in_specs, out_specs=out_specs, check_vma=False)
```

```python
import functools
import math

import jax
import jax.numpy as jnp
from jax import lax
from jax.experimental import pallas as pl
from jax.experimental.pallas import tpu as pltpu
from jax.sharding import PartitionSpec as P

ALPHA = 0.1
BETA_A = math.log(1.0 + 0.5 / 3.0)
BETA_B = math.log(1.0 + 0.5 / 4.0)
MESH = pl.DeviceIdType.MESH
F32 = jnp.float32
BF16 = jnp.bfloat16

NY = 8
NW = 16
NX = 4
CAP = 8
TILE = 128
H = 128
BATCH = 256
SHARD = 2048
RB = 2
NB = 8
NZ = 8
CORES = 2
FAR = (4, 3, 5, 2, 6, 1, 7, 0)
W_ORDER = (8, 7, 9, 6, 10, 5, 11, 4, 12, 3, 13, 2, 14, 1, 15)
X_ORDER = (2, 1, 3)
CHUNK = 4
ROWS = NY * CAP * CHUNK
WAVES = 4


def hops(pair):
    j, ky = pair
    dz, dy = min(FAR[j], NZ - FAR[j]), min(ky, NY - ky)
    return -max(dz, dy), -dz - dy


def schedule():
    steps, left = [], []
    for c, some in enumerate((8, 6, 6, 64)):
        left = sorted(left + [(j, ky) for j in (2 * c, 2 * c + 1) for ky in FAR], key=hops)
        steps.append(left[:some])
        left = left[some:]
    return steps


STEPS = schedule()
ORDER = [pair for step in STEPS for pair in step]
WAVE = {pair: i * WAVES // len(ORDER) for i, pair in enumerate(ORDER)}
PARTS = 8
BLOCK = SHARD // PARTS
VMEM = 40 * 2**20


def fill(ref, sem):
    pltpu.make_async_copy(ref, ref, sem).wait()


def dot(lhs, rhs):
    return jnp.dot(lhs, rhs, preferred_element_type=F32)


def dot_t(lhs, rhs):
    return lax.dot_general(lhs, rhs, (((0,), (0,)), ((), ())), preferred_element_type=F32)


def kernel(
    halo_rows,
    halo_count,
    batch_rows,
    adj_cols,
    hist_in,
    hist_mid,
    current,
    initial,
    upstream,
    adj,
    weight_a,
    weight_b,
    final_out,
    new_in,
    new_mid,
    grad_a,
    grad_b,
    list_v,
    count_v,
    cols,
    asked_y,
    asked_t,
    ask_row,
    asked_w,
    hist,
    onehot,
    rows_out,
    halo,
    tiles,
    adj_v,
    cur_all,
    fresh_all,
    br_all,
    refresh,
    base_mid,
    init_v,
    up_v,
    wa_v,
    wb_v,
    f_fwd,
    f_bwd,
    part,
    sum_w,
    sum_y,
    sum_x,
    total,
    load_sem,
    y_sem,
    w_sem,
    h_send,
    h_recv,
    rep_sem,
    red_sem,
    ready,
):
    node, x = lax.axis_index("node"), lax.axis_index("rep")
    y, w = node // NW, node % NW
    z, core = w // CORES, w % CORES

    def dev(yy, ww, xx):
        return (yy * NW + ww, xx)

    def send(src, dst, s_sem, r_sem, device):
        pltpu.make_async_remote_copy(
            src_ref=src, dst_ref=dst, send_sem=s_sem, recv_sem=r_sem, device_id=device, device_id_type=MESH
        ).start()

    loads = [
        (halo_rows, list_v),
        (halo_count, count_v),
        (batch_rows, br_all.at[x]),
        (adj_cols, cols),
        (hist_in, hist.at[:, pl.ds(0, H)]),
        (hist_mid, hist.at[:, pl.ds(H, H)]),
        (current, cur_all.at[x]),
        (adj, adj_v),
        (initial, init_v),
        (upstream, up_v),
        (weight_a, wa_v),
        (weight_b, wb_v),
    ]
    copies = [pltpu.make_async_copy(s, d, load_sem.at[i]) for i, (s, d) in enumerate(loads)]
    for c in copies:
        c.start()

    barrier = pltpu.get_barrier_semaphore()
    for k in FAR[:-1]:
        pl.semaphore_signal(barrier, inc=1, device_id=dev((y + k) % NY, w, x), device_id_type=MESH)
    for k in W_ORDER:
        pl.semaphore_signal(barrier, inc=1, device_id=dev(y, (w + k) % NW, x), device_id_type=MESH)
    for k in range(1, NX):
        pl.semaphore_signal(barrier, inc=1, device_id=dev(y, w, (x + k) % NX), device_id_type=MESH)

    slot = lax.broadcasted_iota(jnp.int32, (CAP, NY * NW), 0)
    copies[0].wait()
    copies[1].wait()
    asked_y[y] = jnp.where(slot < count_v[...], list_v[...], -1)
    pl.semaphore_wait(barrier, NY + NW + NX - 3)

    for k in FAR[:-1]:
        send(asked_y.at[y], asked_y.at[y], y_sem.at[0], y_sem.at[1], dev((y + k) % NY, w, x))
    fill(asked_y.at[pl.ds(0, NY - 1)], y_sem.at[1])
    lists = asked_y[...].reshape(NY * CAP, NY * NW)
    lists = jnp.concatenate([lists, jnp.zeros((128 - NY * CAP, NY * NW), jnp.int32)], 0)
    asked_t[...] = lists.T
    mine = asked_t[pl.ds(pl.multiple_of(y * NW, NW), NW), :]
    for i in range(NW):
        ask_row[i] = mine[i : i + 1, :]
    for j, k in enumerate(FAR):
        for other in range(CORES):
            if k or other:
                to = (z + NZ - k) % NZ * CORES + (core + other) % CORES
                send(ask_row.at[to], asked_w.at[CORES * j + core], w_sem.at[0], w_sem.at[1], dev(y, to, x))
    asked_w[NW - CORES + core] = ask_row[w]

    copies[2].wait()
    copies[6].wait()
    for k in X_ORDER:
        to = dev(y, w, (x + k) % NX)
        send(br_all.at[x], br_all.at[x], rep_sem.at[0], rep_sem.at[1], to)
        send(cur_all.at[x], cur_all.at[x], rep_sem.at[2], rep_sem.at[3], to)

    fill(asked_w.at[pl.ds(0, NW - 1)], w_sem.at[1])
    wanted = jnp.concatenate([asked_w[i] for i in range(NW)] + [jnp.zeros((128 - NW, 128), jnp.int32)], 0)
    asked_t[...] = wanted.T
    wanted = asked_t[pl.ds(0, NY * CAP), :]
    lane = lax.broadcasted_iota(jnp.int32, (NY * CAP, SHARD), 1)
    for c in range(NW // CHUNK):
        for q in range(CHUNK):
            i = c * CHUNK + q
            hit = jnp.broadcast_to(wanted[:, i : i + 1], (NY * CAP, SHARD)) == lane
            onehot[pl.ds(q * NY * CAP, NY * CAP), :] = hit.astype(F32).astype(BF16)
        if c == 0:
            copies[4].wait()
            copies[5].wait()
        got = dot(onehot[...], hist[...])
        both = jnp.concatenate(
            [got[:, :H].reshape(CHUNK * NY, CAP, H), got[:, H:].reshape(CHUNK * NY, CAP, H)], 1
        )
        rows_out[pl.ds(c * CHUNK, CHUNK)] = both.astype(BF16).reshape(CHUNK, NY, 2 * CAP, H)
        for j, ky in STEPS[c]:
            for other in range(CORES):
                if FAR[j] or ky or other:
                    to_core, to_y = (core + other) % CORES, (y + ky) % NY
                    to_w = (z + FAR[j]) % NZ * CORES + to_core
                    src = rows_out.at[CORES * j + to_core, to_y]
                    dst = halo.at[(j * NY + y) * CORES + core]
                    send(src, dst, h_send, h_recv.at[WAVE[j, ky]], dev(to_y, to_w, x))
    halo[((NZ - 1) * NY + y) * CORES + core] = rows_out[NW - CORES + core, y]

    copies[3].wait()
    copies[7].wait()
    for r in range(RB):
        for c in range(RB):
            acc = jnp.zeros((TILE, TILE), F32)
            for k in range(NB):
                acc = acc + jnp.where(cols[r, k] == c, adj_v[r, k].astype(F32), 0.0)
            high = acc.astype(BF16)
            low = (acc - high.astype(F32)).astype(BF16)
            rs, cs = pl.ds(r * TILE, TILE), pl.ds(c * TILE, TILE)
            f_fwd[rs, cs] = high
            f_fwd[rs, pl.ds(BATCH + c * TILE, TILE)] = low
            acc_t = acc.T
            high_t = acc_t.astype(BF16)
            f_bwd[cs, rs] = high_t
            f_bwd[cs, pl.ds(BATCH + r * TILE, TILE)] = (acc_t - high_t.astype(F32)).astype(BF16)
    for c in range(RB):
        tiles[c, :, pl.ds(0, H)] = cur_all[x, pl.ds(c * TILE, TILE), :]
        tiles[c, :, pl.ds(H, H)] = jnp.zeros((TILE, H), BF16)

    fill(br_all.at[pl.ds(0, NX - 1)], rep_sem.at[1])
    fill(cur_all.at[pl.ds(0, NX - 1)], rep_sem.at[3])
    for p in range(PARTS):
        rows = pl.ds(p * BLOCK, BLOCK)
        row = p * BLOCK + lax.broadcasted_iota(jnp.int32, (BLOCK, BATCH), 0)
        for r in range(NX):
            refresh[rows, pl.ds(r * BATCH, BATCH)] = (br_all[r] == row).astype(F32).astype(BF16)
    new_rows = jnp.concatenate([cur_all[...].reshape(NX * BATCH, H), jnp.ones((NX * BATCH, H), BF16)], 1)
    for p in range(PARTS):
        rows = pl.ds(p * BLOCK, BLOCK)
        put = dot(refresh[rows, :], new_rows)
        kept = put[:, H:] == 0.0
        new_in[rows, :] = jnp.where(kept, hist[rows, pl.ds(0, H)].astype(F32), put[:, :H]).astype(BF16)
        base_mid[rows, :] = jnp.where(kept, hist[rows, pl.ds(H, H)].astype(F32), 0.0).astype(BF16)
    for c in copies[8:]:
        c.wait()

    for wave in range(WAVES):
        pairs = [pair for pair in ORDER if WAVE[pair] == wave]
        fill(halo.at[pl.ds(0, len(pairs) * CORES - (1 if (NZ - 1, 0) in pairs else 0))], h_recv.at[wave])
        for j, ky in pairs:
            yy, zz = (y + NY - ky) % NY, (z + NZ - FAR[j]) % NZ
            block = halo[pl.ds((j * NY + yy) * CORES, CORES)].astype(F32)
            both = [block[:, :CAP, :].reshape(CORES * CAP, H), block[:, CAP:, :].reshape(CORES * CAP, H)]
            rows = pl.ds(pl.multiple_of(zz * CORES * CAP, CORES * CAP), CORES * CAP)
            tiles[RB + yy, rows, :] = jnp.concatenate(both, 1).astype(BF16)
    for k in X_ORDER:
        pl.semaphore_signal(ready, inc=1, device_id=dev(y, w, (x + k) % NX), device_id_type=MESH)

    sums = []
    for r in range(RB):
        left = jnp.concatenate([adj_v[r, k] for k in range(NB)], 1)
        right = jnp.concatenate([tiles[cols[r, k]] for k in range(NB)], 0)
        sums.append(dot(left, right))
    agg = jnp.concatenate(sums, 0)
    init = ALPHA * init_v[...].astype(F32)
    support_a = ((1.0 - ALPHA) * agg[:, :H] + init).astype(BF16)
    preact_a = (1.0 - BETA_A) * support_a.astype(F32) + BETA_A * dot(support_a, wa_v[...])
    fresh = jnp.maximum(preact_a, 0.0).astype(BF16)
    fresh_all[x] = fresh
    for k in X_ORDER:
        send(fresh_all.at[x], fresh_all.at[x], rep_sem.at[4], rep_sem.at[5], dev(y, w, (x + k) % NX))
    agg_b = agg[:, H:] + dot(f_fwd[...], jnp.concatenate([fresh, fresh], 0))
    support_b = ((1.0 - ALPHA) * agg_b + init).astype(BF16)
    preact_b = (1.0 - BETA_B) * support_b.astype(F32) + BETA_B * dot(support_b, wb_v[...])
    final_out[...] = jnp.maximum(preact_b, 0.0).astype(BF16)
    gated_b = jnp.where(preact_b > 0, up_v[...].astype(F32), 0.0).astype(BF16)
    part[pl.ds(H, H), :] = (BETA_B * dot_t(support_b, gated_b)).astype(BF16)
    back = lax.dot_general(gated_b, wb_v[...], (((1,), (1,)), ((), ())), preferred_element_type=F32)
    support_grad = (1.0 - BETA_B) * gated_b.astype(F32) + BETA_B * back
    agg_grad = ((1.0 - ALPHA) * support_grad).astype(BF16)
    fresh_grad = dot(f_bwd[...], jnp.concatenate([agg_grad, agg_grad], 0))
    gated_a = jnp.where(preact_a > 0, fresh_grad, 0.0).astype(BF16)
    part[pl.ds(0, H), :] = (BETA_A * dot_t(support_a, gated_a)).astype(BF16)

    piece = 2 * H // NW
    for k in W_ORDER:
        to = (w + k) % NW
        rows = pl.ds(pl.multiple_of(to * piece, piece), piece)
        send(part.at[rows, :], sum_w.at[w], red_sem.at[0], red_sem.at[1], dev(y, to, x))
    sum_w[w] = part[pl.ds(pl.multiple_of(w * piece, piece), piece), :]
    fill(sum_w.at[pl.ds(0, NW - 1)], red_sem.at[1])
    sum_y[y] = jnp.sum(sum_w[...].astype(F32), 0)
    for k in FAR[:-1]:
        send(sum_y.at[y], sum_y.at[y], red_sem.at[2], red_sem.at[3], dev((y + k) % NY, w, x))
    fill(sum_y.at[pl.ds(0, NY - 1)], red_sem.at[3])
    sum_x[x] = jnp.sum(sum_y[...], 0)
    for k in X_ORDER:
        send(sum_x.at[x], sum_x.at[x], red_sem.at[4], red_sem.at[5], dev(y, w, (x + k) % NX))
    fill(sum_x.at[pl.ds(0, NX - 1)], red_sem.at[5])
    total[w] = (jnp.sum(sum_x[...], 0) * (1.0 / math.sqrt(NY * NW * NX * BATCH))).astype(BF16)
    for k in W_ORDER:
        send(total.at[w], total.at[w], red_sem.at[6], red_sem.at[7], dev(y, (w + k) % NW, x))

    pl.semaphore_wait(ready, NX - 1)
    fill(fresh_all.at[pl.ds(0, NX - 1)], rep_sem.at[5])
    fresh_rows = fresh_all[...].reshape(NX * BATCH, H)
    for p in range(PARTS):
        rows = pl.ds(p * BLOCK, BLOCK)
        put = dot(refresh[rows, :], fresh_rows)
        new_mid[rows, :] = (put + base_mid[rows, :].astype(F32)).astype(BF16)

    fill(total.at[pl.ds(0, NW - 1)], red_sem.at[7])
    half = NW // 2
    grad_a[...] = total[pl.ds(0, half)].astype(F32).reshape(H, H)
    grad_b[...] = total[pl.ds(half, half)].astype(F32).reshape(H, H)

    fill(asked_y.at[pl.ds(0, NY - 1)], y_sem.at[0])
    fill(asked_w.at[pl.ds(0, NW - 1)], w_sem.at[0])
    fill(br_all.at[pl.ds(0, NX - 1)], rep_sem.at[0])
    fill(cur_all.at[pl.ds(0, NX - 1)], rep_sem.at[2])
    fill(fresh_all.at[pl.ds(0, NX - 1)], rep_sem.at[4])
    fill(halo.at[pl.ds(0, NY * NW - 1)], h_send)
    fill(sum_w.at[pl.ds(0, NW - 1)], red_sem.at[0])
    fill(sum_y.at[pl.ds(0, NY - 1)], red_sem.at[2])
    fill(sum_x.at[pl.ds(0, NX - 1)], red_sem.at[4])
    fill(total.at[pl.ds(0, NW - 1)], red_sem.at[6])


def write_out(*refs):
    sems = refs[-1]
    copies = [pltpu.make_async_copy(refs[i], refs[5 + i], sems.at[i]) for i in range(5)]
    for c in copies:
        c.start()
    for c in copies:
        c.wait()


def on_device(
    history_in,
    history_mid,
    current,
    initial,
    batch_rows,
    halo_rows,
    halo_count,
    adj_cols,
    adj_vals,
    upstream,
    weight_a,
    weight_b,
):
    vmem = pl.BlockSpec(memory_space=pltpu.VMEM)
    hbm = pl.BlockSpec(memory_space=pltpu.HBM)
    sds = jax.ShapeDtypeStruct
    dma = pltpu.SemaphoreType.DMA
    piece = 2 * H // NW
    results = pl.pallas_call(
        kernel,
        name="gcn",
        out_shape=(
            sds((BATCH, H), BF16),
            sds((SHARD, H), BF16),
            sds((SHARD, H), BF16),
            sds((H, H), F32),
            sds((H, H), F32),
        ),
        in_specs=[hbm] * 12,
        out_specs=(vmem,) * 5,
        scratch_shapes=[
            pltpu.VMEM((CAP, NY * NW), jnp.int32),
            pltpu.VMEM((1, NY * NW), jnp.int32),
            pltpu.SMEM((RB, NB), jnp.int32),
            pltpu.VMEM((NY, CAP, NY * NW), jnp.int32),
            pltpu.VMEM((128, 128), jnp.int32),
            pltpu.VMEM((NW, 1, 128), jnp.int32),
            pltpu.VMEM((NW, 1, 128), jnp.int32),
            pltpu.VMEM((SHARD, 2 * H), BF16),
            pltpu.VMEM((ROWS, SHARD), BF16),
            pltpu.VMEM((NW, NY, 2 * CAP, H), BF16),
            pltpu.VMEM((NY * NW, 2 * CAP, H), BF16),
            pltpu.VMEM((RB + NY, TILE, 2 * H), BF16),
            pltpu.VMEM((RB, NB, TILE, TILE), BF16),
            pltpu.VMEM((NX, BATCH, H), BF16),
            pltpu.VMEM((NX, BATCH, H), BF16),
            pltpu.VMEM((NX, 1, BATCH), jnp.int32),
            pltpu.VMEM((SHARD, NX * BATCH), BF16),
            pltpu.VMEM((SHARD, H), BF16),
            pltpu.VMEM((BATCH, H), BF16),
            pltpu.VMEM((BATCH, H), BF16),
            pltpu.VMEM((H, H), BF16),
            pltpu.VMEM((H, H), BF16),
            pltpu.VMEM((BATCH, 2 * BATCH), BF16),
            pltpu.VMEM((BATCH, 2 * BATCH), BF16),
            pltpu.VMEM((2 * H, H), BF16),
            pltpu.VMEM((NW, piece, H), BF16),
            pltpu.VMEM((NY, piece, H), F32),
            pltpu.VMEM((NX, piece, H), F32),
            pltpu.VMEM((NW, piece, H), BF16),
            dma((12,)),
            dma((2,)),
            dma((2,)),
            dma,
            dma((WAVES,)),
            dma((6,)),
            dma((8,)),
            pltpu.SemaphoreType.REGULAR,
        ],
        compiler_params=pltpu.CompilerParams(
            collective_id=0, has_side_effects=True, vmem_limit_bytes=VMEM
        ),
    )(*[pltpu.with_memory_space_constraint(a, pltpu.HBM) for a in (
        halo_rows[0].T,
        halo_count,
        batch_rows[None, :],
        adj_cols[0],
        history_in,
        history_mid,
        current,
        initial,
        upstream,
        adj_vals[0],
        weight_a,
        weight_b,
    )])
    return pl.pallas_call(
        write_out,
        name="write_out",
        out_shape=tuple(sds(r.shape, r.dtype) for r in results),
        in_specs=[vmem] * 5,
        out_specs=(hbm,) * 5,
        scratch_shapes=[dma((5,))],
        compiler_params=pltpu.CompilerParams(vmem_limit_bytes=4 * 2**20),
    )(*results)


def solution(mesh):
    both = ("node", "rep")
    in_specs = (
        P("node", None),
        P("node", None),
        P(both, None),
        P(both, None),
        P(both),
        P(both, None, None),
        P(both, None),
        P(both, None, None),
        P(both, None, None, None, None),
        P(both, None),
        P(),
        P(),
    )
    out_specs = (P(both, None), P("node", None), P("node", None), P(), P())
    return jax.shard_map(on_device, mesh=mesh, in_specs=in_specs, out_specs=out_specs, check_vma=False)
```

```python
import math

import jax
import jax.numpy as jnp
from jax import lax
from jax.experimental import pallas as pl
from jax.experimental.pallas import tpu as pltpu
from jax.sharding import PartitionSpec as P

ALPHA = 0.1
BETA_A = math.log(1.0 + 0.5 / 3.0)
BETA_B = math.log(1.0 + 0.5 / 4.0)
MESH = pl.DeviceIdType.MESH
F32 = jnp.float32
BF16 = jnp.bfloat16

NY = 8
NW = 16
NX = 4
CAP = 8
TILE = 128
H = 128
BATCH = 256
SHARD = 2048
RB = 2
NB = 8
NZ = 8
CORES = 2
FAR = (4, 3, 5, 2, 6, 1, 7, 0)
W_ORDER = (8, 7, 9, 6, 10, 5, 11, 4, 12, 3, 13, 2, 14, 1, 15)
X_ORDER = (2, 1, 3)
CHUNK = 4
ROWS = NY * CAP * CHUNK
WAVES = 4
GROUP = NX * CORES
PIECE = 2 * H // GROUP
SCALE = 1.0 / math.sqrt(NY * NW * NX * BATCH)


def hops(pair):
    j, ky = pair
    dz, dy = min(FAR[j], NZ - FAR[j]), min(ky, NY - ky)
    return -max(dz, dy), -dz - dy


def schedule():
    steps, left = [], []
    for c, some in enumerate((8, 6, 6, 64)):
        left = sorted(left + [(j, ky) for j in (2 * c, 2 * c + 1) for ky in FAR], key=hops)
        steps.append(left[:some])
        left = left[some:]
    return steps


STEPS = schedule()
ORDER = [pair for step in STEPS for pair in step]
WAVE = {pair: i * WAVES // len(ORDER) for i, pair in enumerate(ORDER)}
PARTS = 8
BLOCK = SHARD // PARTS
VMEM = 40 * 2**20


def fill(ref, sem):
    pltpu.make_async_copy(ref, ref, sem).wait()


def dot(lhs, rhs):
    return jnp.dot(lhs, rhs, preferred_element_type=F32)


def dot_t(lhs, rhs):
    return lax.dot_general(lhs, rhs, (((0,), (0,)), ((), ())), preferred_element_type=F32)


def kernel(
    halo_rows,
    halo_count,
    batch_rows,
    adj_cols,
    hist_in,
    hist_mid,
    current,
    initial,
    upstream,
    adj,
    weight_a,
    weight_b,
    final_out,
    new_in,
    new_mid,
    grad_a,
    grad_b,
    list_v,
    count_v,
    cols,
    asked_y,
    asked_t,
    ask_row,
    asked_w,
    hist,
    onehot,
    rows_out,
    halo,
    tiles,
    adj_v,
    cur_all,
    fresh_all,
    br_all,
    refresh,
    base_mid,
    init_v,
    up_v,
    wa_v,
    wb_v,
    f_fwd,
    f_bwd,
    part,
    sum_g,
    sum_z,
    sum_y,
    total,
    load_sem,
    y_sem,
    w_sem,
    h_send,
    h_recv,
    rep_sem,
    red_sem,
):
    node, x = lax.axis_index("node"), lax.axis_index("rep")
    y, w = node // NW, node % NW
    z, core = w // CORES, w % CORES

    def dev(yy, ww, xx):
        return (yy * NW + ww, xx)

    def send(src, dst, s_sem, r_sem, device):
        pltpu.make_async_remote_copy(
            src_ref=src, dst_ref=dst, send_sem=s_sem, recv_sem=r_sem, device_id=device, device_id_type=MESH
        ).start()

    loads = [
        (halo_rows, list_v),
        (halo_count, count_v),
        (batch_rows, br_all.at[x]),
        (adj_cols, cols),
        (hist_in, hist.at[:, pl.ds(0, H)]),
        (hist_mid, hist.at[:, pl.ds(H, H)]),
        (current, cur_all.at[x]),
        (adj, adj_v),
        (initial, init_v),
        (upstream, up_v),
        (weight_a, wa_v),
        (weight_b, wb_v),
    ]
    copies = [pltpu.make_async_copy(s, d, load_sem.at[i]) for i, (s, d) in enumerate(loads)]
    for c in copies:
        c.start()

    barrier = pltpu.get_barrier_semaphore()
    for k in FAR[:-1]:
        pl.semaphore_signal(barrier, inc=1, device_id=dev((y + k) % NY, w, x), device_id_type=MESH)
    for k in W_ORDER:
        pl.semaphore_signal(barrier, inc=1, device_id=dev(y, (w + k) % NW, x), device_id_type=MESH)
    for k in range(1, NX):
        pl.semaphore_signal(barrier, inc=1, device_id=dev(y, w, (x + k) % NX), device_id_type=MESH)

    slot = lax.broadcasted_iota(jnp.int32, (CAP, NY * NW), 0)
    copies[0].wait()
    copies[1].wait()
    asked_y[y] = jnp.where(slot < count_v[...], list_v[...], -1)
    pl.semaphore_wait(barrier, NY + NW + NX - 3)

    for k in FAR[:-1]:
        send(asked_y.at[y], asked_y.at[y], y_sem.at[0], y_sem.at[1], dev((y + k) % NY, w, x))
    fill(asked_y.at[pl.ds(0, NY - 1)], y_sem.at[1])
    lists = asked_y[...].reshape(NY * CAP, NY * NW)
    lists = jnp.concatenate([lists, jnp.zeros((128 - NY * CAP, NY * NW), jnp.int32)], 0)
    asked_t[...] = lists.T
    mine = asked_t[pl.ds(pl.multiple_of(y * NW, NW), NW), :]
    for i in range(NW):
        ask_row[i] = mine[i : i + 1, :]
    for j, k in enumerate(FAR):
        for other in range(CORES):
            if k or other:
                to = (z + NZ - k) % NZ * CORES + (core + other) % CORES
                send(ask_row.at[to], asked_w.at[CORES * j + core], w_sem.at[0], w_sem.at[1], dev(y, to, x))
    asked_w[NW - CORES + core] = ask_row[w]

    copies[2].wait()
    copies[6].wait()
    for k in X_ORDER:
        to = dev(y, w, (x + k) % NX)
        send(br_all.at[x], br_all.at[x], rep_sem.at[0], rep_sem.at[1], to)
        send(cur_all.at[x], cur_all.at[x], rep_sem.at[2], rep_sem.at[3], to)

    fill(asked_w.at[pl.ds(0, NW - 1)], w_sem.at[1])
    wanted = jnp.concatenate([asked_w[i] for i in range(NW)] + [jnp.zeros((128 - NW, 128), jnp.int32)], 0)
    asked_t[...] = wanted.T
    wanted = asked_t[pl.ds(0, NY * CAP), :]
    lane = lax.broadcasted_iota(jnp.int32, (NY * CAP, SHARD), 1)
    for c in range(NW // CHUNK):
        for q in range(CHUNK):
            i = c * CHUNK + q
            hit = jnp.broadcast_to(wanted[:, i : i + 1], (NY * CAP, SHARD)) == lane
            onehot[pl.ds(q * NY * CAP, NY * CAP), :] = hit.astype(F32).astype(BF16)
        if c == 0:
            copies[4].wait()
            copies[5].wait()
        got = dot(onehot[...], hist[...])
        both = jnp.concatenate(
            [got[:, :H].reshape(CHUNK * NY, CAP, H), got[:, H:].reshape(CHUNK * NY, CAP, H)], 1
        )
        rows_out[pl.ds(c * CHUNK, CHUNK)] = both.astype(BF16).reshape(CHUNK, NY, 2 * CAP, H)
        for j, ky in STEPS[c]:
            for other in range(CORES):
                if FAR[j] or ky or other:
                    to_core, to_y = (core + other) % CORES, (y + ky) % NY
                    to_w = (z + FAR[j]) % NZ * CORES + to_core
                    src = rows_out.at[CORES * j + to_core, to_y]
                    dst = halo.at[(j * NY + y) * CORES + core]
                    send(src, dst, h_send, h_recv.at[WAVE[j, ky]], dev(to_y, to_w, x))
    halo[((NZ - 1) * NY + y) * CORES + core] = rows_out[NW - CORES + core, y]

    copies[3].wait()
    copies[7].wait()
    for r in range(RB):
        for c in range(RB):
            acc = jnp.zeros((TILE, TILE), F32)
            for k in range(NB):
                acc = acc + jnp.where(cols[r, k] == c, adj_v[r, k].astype(F32), 0.0)
            high = acc.astype(BF16)
            low = (acc - high.astype(F32)).astype(BF16)
            rs, cs = pl.ds(r * TILE, TILE), pl.ds(c * TILE, TILE)
            f_fwd[rs, cs] = high
            f_fwd[rs, pl.ds(BATCH + c * TILE, TILE)] = low
            acc_t = acc.T
            high_t = acc_t.astype(BF16)
            f_bwd[cs, rs] = high_t
            f_bwd[cs, pl.ds(BATCH + r * TILE, TILE)] = (acc_t - high_t.astype(F32)).astype(BF16)
    for c in range(RB):
        tiles[c, :, pl.ds(0, H)] = cur_all[x, pl.ds(c * TILE, TILE), :]
        tiles[c, :, pl.ds(H, H)] = jnp.zeros((TILE, H), BF16)

    fill(br_all.at[pl.ds(0, NX - 1)], rep_sem.at[1])
    fill(cur_all.at[pl.ds(0, NX - 1)], rep_sem.at[3])
    for p in range(PARTS):
        rows = pl.ds(p * BLOCK, BLOCK)
        row = p * BLOCK + lax.broadcasted_iota(jnp.int32, (BLOCK, BATCH), 0)
        for r in range(NX):
            refresh[rows, pl.ds(r * BATCH, BATCH)] = (br_all[r] == row).astype(F32).astype(BF16)
    new_rows = jnp.concatenate([cur_all[...].reshape(NX * BATCH, H), jnp.ones((NX * BATCH, H), BF16)], 1)
    for p in range(PARTS):
        rows = pl.ds(p * BLOCK, BLOCK)
        put = dot(refresh[rows, :], new_rows)
        kept = put[:, H:] == 0.0
        new_in[rows, :] = jnp.where(kept, hist[rows, pl.ds(0, H)].astype(F32), put[:, :H]).astype(BF16)
        base_mid[rows, :] = jnp.where(kept, hist[rows, pl.ds(H, H)].astype(F32), 0.0).astype(BF16)
    for c in copies[8:]:
        c.wait()

    for wave in range(WAVES):
        pairs = [pair for pair in ORDER if WAVE[pair] == wave]
        fill(halo.at[pl.ds(0, len(pairs) * CORES - (1 if (NZ - 1, 0) in pairs else 0))], h_recv.at[wave])
        for j, ky in pairs:
            yy, zz = (y + NY - ky) % NY, (z + NZ - FAR[j]) % NZ
            block = halo[pl.ds((j * NY + yy) * CORES, CORES)].astype(F32)
            both = [block[:, :CAP, :].reshape(CORES * CAP, H), block[:, CAP:, :].reshape(CORES * CAP, H)]
            rows = pl.ds(pl.multiple_of(zz * CORES * CAP, CORES * CAP), CORES * CAP)
            tiles[RB + yy, rows, :] = jnp.concatenate(both, 1).astype(BF16)

    sums = []
    for r in range(RB):
        left = jnp.concatenate([adj_v[r, k] for k in range(NB)], 1)
        right = jnp.concatenate([tiles[cols[r, k]] for k in range(NB)], 0)
        sums.append(dot(left, right))
    agg = jnp.concatenate(sums, 0)
    init = ALPHA * init_v[...].astype(F32)
    support_a = ((1.0 - ALPHA) * agg[:, :H] + init).astype(BF16)
    preact_a = (1.0 - BETA_A) * support_a.astype(F32) + BETA_A * dot(support_a, wa_v[...])
    fresh = jnp.maximum(preact_a, 0.0).astype(BF16)
    fresh_all[x] = fresh
    agg_b = agg[:, H:] + dot(f_fwd[...], jnp.concatenate([fresh, fresh], 0))
    support_b = ((1.0 - ALPHA) * agg_b + init).astype(BF16)
    preact_b = (1.0 - BETA_B) * support_b.astype(F32) + BETA_B * dot(support_b, wb_v[...])
    final_out[...] = jnp.maximum(preact_b, 0.0).astype(BF16)
    gated_b = jnp.where(preact_b > 0, up_v[...].astype(F32), 0.0).astype(BF16)
    part[pl.ds(H, H), :] = (BETA_B * dot_t(support_b, gated_b)).astype(BF16)
    back = lax.dot_general(gated_b, wb_v[...], (((1,), (1,)), ((), ())), preferred_element_type=F32)
    support_grad = (1.0 - BETA_B) * gated_b.astype(F32) + BETA_B * back
    agg_grad = ((1.0 - ALPHA) * support_grad).astype(BF16)
    fresh_grad = dot(f_bwd[...], jnp.concatenate([agg_grad, agg_grad], 0))
    gated_a = jnp.where(preact_a > 0, fresh_grad, 0.0).astype(BF16)
    part[pl.ds(0, H), :] = (BETA_A * dot_t(support_a, gated_a)).astype(BF16)

    group = x * CORES + core
    friends = []
    for k in X_ORDER + (0,):
        for other in range(CORES):
            if k or other:
                to_x, to_core = (x + k) % NX, (core + other) % CORES
                friends.append((to_x * CORES + to_core, dev(y, z * CORES + to_core, to_x)))
    for to, device in friends:
        rows = pl.ds(pl.multiple_of(to * PIECE, PIECE), PIECE)
        send(part.at[rows, :], sum_g.at[group], red_sem.at[0], red_sem.at[1], device)
    sum_g[group] = part[pl.ds(pl.multiple_of(group * PIECE, PIECE), PIECE), :]
    fill(sum_g.at[pl.ds(0, GROUP - 1)], red_sem.at[1])
    sum_z[z] = jnp.sum(sum_g[...].astype(F32), 0).astype(BF16)
    for k in FAR[:-1]:
        to = (z + k) % NZ * CORES + core
        send(sum_z.at[z], sum_z.at[z], red_sem.at[2], red_sem.at[3], dev(y, to, x))
    for k in X_ORDER:
        send(fresh_all.at[x], fresh_all.at[x], rep_sem.at[4], rep_sem.at[5], dev(y, w, (x + k) % NX))
    fill(sum_z.at[pl.ds(0, NZ - 1)], red_sem.at[3])
    sum_y[y] = jnp.sum(sum_z[...].astype(F32), 0).astype(BF16)
    for k in FAR[:-1]:
        send(sum_y.at[y], sum_y.at[y], red_sem.at[4], red_sem.at[5], dev((y + k) % NY, w, x))
    fill(sum_y.at[pl.ds(0, NY - 1)], red_sem.at[5])
    total[group] = (jnp.sum(sum_y[...].astype(F32), 0) * SCALE).astype(BF16)
    for _, device in friends:
        send(total.at[group], total.at[group], red_sem.at[6], red_sem.at[7], device)

    fill(fresh_all.at[pl.ds(0, NX - 1)], rep_sem.at[5])
    fresh_rows = fresh_all[...].reshape(NX * BATCH, H)
    for p in range(PARTS):
        rows = pl.ds(p * BLOCK, BLOCK)
        put = dot(refresh[rows, :], fresh_rows)
        new_mid[rows, :] = (put + base_mid[rows, :].astype(F32)).astype(BF16)

    fill(total.at[pl.ds(0, GROUP - 1)], red_sem.at[7])
    half = GROUP // 2
    grad_a[...] = total[pl.ds(0, half)].astype(F32).reshape(H, H)
    grad_b[...] = total[pl.ds(half, half)].astype(F32).reshape(H, H)

    fill(asked_y.at[pl.ds(0, NY - 1)], y_sem.at[0])
    fill(asked_w.at[pl.ds(0, NW - 1)], w_sem.at[0])
    fill(br_all.at[pl.ds(0, NX - 1)], rep_sem.at[0])
    fill(cur_all.at[pl.ds(0, NX - 1)], rep_sem.at[2])
    fill(fresh_all.at[pl.ds(0, NX - 1)], rep_sem.at[4])
    fill(halo.at[pl.ds(0, NY * NW - 1)], h_send)
    fill(sum_g.at[pl.ds(0, GROUP - 1)], red_sem.at[0])
    fill(sum_z.at[pl.ds(0, NZ - 1)], red_sem.at[2])
    fill(sum_y.at[pl.ds(0, NY - 1)], red_sem.at[4])
    fill(total.at[pl.ds(0, GROUP - 1)], red_sem.at[6])


def write_out(*refs):
    sems = refs[-1]
    copies = [pltpu.make_async_copy(refs[i], refs[5 + i], sems.at[i]) for i in range(5)]
    for c in copies:
        c.start()
    for c in copies:
        c.wait()


def on_device(
    history_in,
    history_mid,
    current,
    initial,
    batch_rows,
    halo_rows,
    halo_count,
    adj_cols,
    adj_vals,
    upstream,
    weight_a,
    weight_b,
):
    vmem = pl.BlockSpec(memory_space=pltpu.VMEM)
    hbm = pl.BlockSpec(memory_space=pltpu.HBM)
    sds = jax.ShapeDtypeStruct
    dma = pltpu.SemaphoreType.DMA
    results = pl.pallas_call(
        kernel,
        name="gcn",
        out_shape=(
            sds((BATCH, H), BF16),
            sds((SHARD, H), BF16),
            sds((SHARD, H), BF16),
            sds((H, H), F32),
            sds((H, H), F32),
        ),
        in_specs=[hbm] * 12,
        out_specs=(vmem,) * 5,
        scratch_shapes=[
            pltpu.VMEM((CAP, NY * NW), jnp.int32),
            pltpu.VMEM((1, NY * NW), jnp.int32),
            pltpu.SMEM((RB, NB), jnp.int32),
            pltpu.VMEM((NY, CAP, NY * NW), jnp.int32),
            pltpu.VMEM((128, 128), jnp.int32),
            pltpu.VMEM((NW, 1, 128), jnp.int32),
            pltpu.VMEM((NW, 1, 128), jnp.int32),
            pltpu.VMEM((SHARD, 2 * H), BF16),
            pltpu.VMEM((ROWS, SHARD), BF16),
            pltpu.VMEM((NW, NY, 2 * CAP, H), BF16),
            pltpu.VMEM((NY * NW, 2 * CAP, H), BF16),
            pltpu.VMEM((RB + NY, TILE, 2 * H), BF16),
            pltpu.VMEM((RB, NB, TILE, TILE), BF16),
            pltpu.VMEM((NX, BATCH, H), BF16),
            pltpu.VMEM((NX, BATCH, H), BF16),
            pltpu.VMEM((NX, 1, BATCH), jnp.int32),
            pltpu.VMEM((SHARD, NX * BATCH), BF16),
            pltpu.VMEM((SHARD, H), BF16),
            pltpu.VMEM((BATCH, H), BF16),
            pltpu.VMEM((BATCH, H), BF16),
            pltpu.VMEM((H, H), BF16),
            pltpu.VMEM((H, H), BF16),
            pltpu.VMEM((BATCH, 2 * BATCH), BF16),
            pltpu.VMEM((BATCH, 2 * BATCH), BF16),
            pltpu.VMEM((2 * H, H), BF16),
            pltpu.VMEM((GROUP, PIECE, H), BF16),
            pltpu.VMEM((NZ, PIECE, H), BF16),
            pltpu.VMEM((NY, PIECE, H), BF16),
            pltpu.VMEM((GROUP, PIECE, H), BF16),
            dma((12,)),
            dma((2,)),
            dma((2,)),
            dma,
            dma((WAVES,)),
            dma((6,)),
            dma((8,)),
        ],
        compiler_params=pltpu.CompilerParams(
            collective_id=0, has_side_effects=True, vmem_limit_bytes=VMEM
        ),
    )(*[pltpu.with_memory_space_constraint(a, pltpu.HBM) for a in (
        halo_rows[0].T,
        halo_count,
        batch_rows[None, :],
        adj_cols[0],
        history_in,
        history_mid,
        current,
        initial,
        upstream,
        adj_vals[0],
        weight_a,
        weight_b,
    )])
    return pl.pallas_call(
        write_out,
        name="write_out",
        out_shape=tuple(sds(r.shape, r.dtype) for r in results),
        in_specs=[vmem] * 5,
        out_specs=(hbm,) * 5,
        scratch_shapes=[dma((5,))],
        compiler_params=pltpu.CompilerParams(vmem_limit_bytes=4 * 2**20),
    )(*results)


def solution(mesh):
    both = ("node", "rep")
    in_specs = (
        P("node", None),
        P("node", None),
        P(both, None),
        P(both, None),
        P(both),
        P(both, None, None),
        P(both, None),
        P(both, None, None),
        P(both, None, None, None, None),
        P(both, None),
        P(),
        P(),
    )
    out_specs = (P(both, None), P("node", None), P("node", None), P(), P())
    return jax.shard_map(on_device, mesh=mesh, in_specs=in_specs, out_specs=out_specs, check_vma=False)
```

```python
import math

import jax
import jax.numpy as jnp
from jax import lax
from jax.experimental import pallas as pl
from jax.experimental.pallas import tpu as pltpu
from jax.sharding import PartitionSpec as P

ALPHA = 0.1
BETA_A = math.log(1.0 + 0.5 / 3.0)
BETA_B = math.log(1.0 + 0.5 / 4.0)
MESH = pl.DeviceIdType.MESH
F32 = jnp.float32
BF16 = jnp.bfloat16

NY = 8
NW = 16
NX = 4
CAP = 8
TILE = 128
H = 128
BATCH = 256
SHARD = 2048
RB = 2
NB = 8
NZ = 8
CORES = 2
FAR = (4, 3, 5, 2, 6, 1, 7, 0)
W_ORDER = (8, 7, 9, 6, 10, 5, 11, 4, 12, 3, 13, 2, 14, 1, 15)
X_ORDER = (2, 1, 3)
CHUNKS = ((0,), (1,), (2, 3), (4, 5), (6, 7))
ROWS = NY * CAP * CORES * 2
WAVES = 4
GROUP = NX * CORES
PIECE = 2 * H // GROUP
SCALE = 1.0 / math.sqrt(NY * NW * NX * BATCH)


def hops(pair):
    j, ky = pair
    dz, dy = min(FAR[j], NZ - FAR[j]), min(ky, NY - ky)
    return -max(dz, dy), -dz - dy


def schedule():
    steps, left = [], []
    for chunk, some in zip(CHUNKS, (8, 4, 6, 6, 64)):
        left = sorted(left + [(j, ky) for j in chunk for ky in FAR], key=hops)
        steps.append(left[:some])
        left = left[some:]
    return steps


STEPS = schedule()
ORDER = [pair for step in STEPS for pair in step]
WAVE = {pair: i * WAVES // len(ORDER) for i, pair in enumerate(ORDER)}
PARTS = 8
BLOCK = SHARD // PARTS
VMEM = 40 * 2**20


def fill(ref, sem):
    pltpu.make_async_copy(ref, ref, sem).wait()


def dot(lhs, rhs):
    return jnp.dot(lhs, rhs, preferred_element_type=F32)


def dot_t(lhs, rhs):
    return lax.dot_general(lhs, rhs, (((0,), (0,)), ((), ())), preferred_element_type=F32)


def kernel(
    halo_rows,
    halo_count,
    batch_rows,
    adj_cols,
    hist_in,
    hist_mid,
    current,
    initial,
    upstream,
    adj,
    weight_a,
    weight_b,
    final_out,
    new_in,
    new_mid,
    grad_a,
    grad_b,
    list_v,
    count_v,
    cols,
    asked_y,
    asked_t,
    ask_row,
    asked_w,
    hist,
    onehot,
    rows_out,
    halo,
    tiles,
    adj_v,
    cur_all,
    fresh_all,
    br_all,
    refresh,
    base_mid,
    init_v,
    up_v,
    wa_v,
    wb_v,
    f_fwd,
    f_bwd,
    part,
    sum_g,
    sum_z,
    sum_y,
    total,
    load_sem,
    y_sem,
    w_sem,
    h_send,
    h_recv,
    rep_sem,
    red_sem,
):
    node, x = lax.axis_index("node"), lax.axis_index("rep")
    y, w = node // NW, node % NW
    z, core = w // CORES, w % CORES

    def dev(yy, ww, xx):
        return (yy * NW + ww, xx)

    def send(src, dst, s_sem, r_sem, device):
        pltpu.make_async_remote_copy(
            src_ref=src, dst_ref=dst, send_sem=s_sem, recv_sem=r_sem, device_id=device, device_id_type=MESH
        ).start()

    loads = [
        (halo_rows, list_v),
        (halo_count, count_v),
        (batch_rows, br_all.at[x]),
        (adj_cols, cols),
        (hist_in, hist.at[:, pl.ds(0, H)]),
        (hist_mid, hist.at[:, pl.ds(H, H)]),
        (current, cur_all.at[x]),
        (adj, adj_v),
        (initial, init_v),
        (upstream, up_v),
        (weight_a, wa_v),
        (weight_b, wb_v),
    ]
    copies = [pltpu.make_async_copy(s, d, load_sem.at[i]) for i, (s, d) in enumerate(loads)]
    copies[0].start()
    copies[1].start()

    barrier = pltpu.get_barrier_semaphore()
    for k in FAR[:-1]:
        pl.semaphore_signal(barrier, inc=1, device_id=dev((y + k) % NY, w, x), device_id_type=MESH)
    for k in W_ORDER:
        pl.semaphore_signal(barrier, inc=1, device_id=dev(y, (w + k) % NW, x), device_id_type=MESH)
    for k in range(1, NX):
        pl.semaphore_signal(barrier, inc=1, device_id=dev(y, w, (x + k) % NX), device_id_type=MESH)

    slot = lax.broadcasted_iota(jnp.int32, (CAP, NY * NW), 0)
    copies[0].wait()
    copies[1].wait()
    asked_y[y] = jnp.where(slot < count_v[...], list_v[...], -1)
    pl.semaphore_wait(barrier, NY + NW + NX - 3)

    for k in FAR[:-1]:
        send(asked_y.at[y], asked_y.at[y], y_sem.at[0], y_sem.at[1], dev((y + k) % NY, w, x))
    for c in copies[2:]:
        c.start()
    copies[2].wait()
    copies[6].wait()
    for k in X_ORDER:
        to = dev(y, w, (x + k) % NX)
        send(br_all.at[x], br_all.at[x], rep_sem.at[0], rep_sem.at[1], to)
        send(cur_all.at[x], cur_all.at[x], rep_sem.at[2], rep_sem.at[3], to)

    fill(asked_y.at[pl.ds(0, NY - 1)], y_sem.at[1])
    lists = asked_y[...].reshape(NY * CAP, NY * NW)
    lists = jnp.concatenate([lists, jnp.zeros((128 - NY * CAP, NY * NW), jnp.int32)], 0)
    asked_t[...] = lists.T
    mine = asked_t[pl.ds(pl.multiple_of(y * NW, NW), NW), :]
    for i in range(NW):
        ask_row[i] = mine[i : i + 1, :]
    for j, k in enumerate(FAR):
        for other in range(CORES):
            if k or other:
                to = (z + NZ - k) % NZ * CORES + (core + other) % CORES
                send(ask_row.at[to], asked_w.at[CORES * j + core], w_sem.at[0], w_sem.at[1], dev(y, to, x))
    asked_w[NW - CORES + core] = ask_row[w]

    fill(asked_w.at[pl.ds(0, NW - 1)], w_sem.at[1])
    wanted = jnp.concatenate([asked_w[i] for i in range(NW)] + [jnp.zeros((128 - NW, 128), jnp.int32)], 0)
    asked_t[...] = wanted.T
    wanted = asked_t[pl.ds(0, NY * CAP), :]
    lane = lax.broadcasted_iota(jnp.int32, (NY * CAP, SHARD), 1)
    for c, chunk in enumerate(CHUNKS):
        first, lists = chunk[0] * CORES, len(chunk) * CORES
        for q in range(lists):
            hit = jnp.broadcast_to(wanted[:, first + q : first + q + 1], (NY * CAP, SHARD)) == lane
            onehot[pl.ds(q * NY * CAP, NY * CAP), :] = hit.astype(F32).astype(BF16)
        if c == 0:
            copies[4].wait()
            copies[5].wait()
        got = dot(onehot[pl.ds(0, lists * NY * CAP), :], hist[...])
        both = jnp.concatenate([got[:, :H].reshape(lists * NY, CAP, H), got[:, H:].reshape(lists * NY, CAP, H)], 1)
        rows_out[pl.ds(first, lists)] = both.astype(BF16).reshape(lists, NY, 2 * CAP, H)
        for j, ky in STEPS[c]:
            for other in range(CORES):
                if FAR[j] or ky or other:
                    to_core, to_y = (core + other) % CORES, (y + ky) % NY
                    to_w = (z + FAR[j]) % NZ * CORES + to_core
                    src = rows_out.at[CORES * j + to_core, to_y]
                    dst = halo.at[(j * NY + y) * CORES + core]
                    send(src, dst, h_send, h_recv.at[WAVE[j, ky]], dev(to_y, to_w, x))
    halo[((NZ - 1) * NY + y) * CORES + core] = rows_out[NW - CORES + core, y]

    copies[3].wait()
    copies[7].wait()
    for r in range(RB):
        for c in range(RB):
            acc = jnp.zeros((TILE, TILE), F32)
            for k in range(NB):
                acc = acc + jnp.where(cols[r, k] == c, adj_v[r, k].astype(F32), 0.0)
            high = acc.astype(BF16)
            low = (acc - high.astype(F32)).astype(BF16)
            rs, cs = pl.ds(r * TILE, TILE), pl.ds(c * TILE, TILE)
            f_fwd[rs, cs] = high
            f_fwd[rs, pl.ds(BATCH + c * TILE, TILE)] = low
            acc_t = acc.T
            high_t = acc_t.astype(BF16)
            f_bwd[cs, rs] = high_t
            f_bwd[cs, pl.ds(BATCH + r * TILE, TILE)] = (acc_t - high_t.astype(F32)).astype(BF16)
    for c in range(RB):
        tiles[c, :, pl.ds(0, H)] = cur_all[x, pl.ds(c * TILE, TILE), :]
        tiles[c, :, pl.ds(H, H)] = jnp.zeros((TILE, H), BF16)

    fill(br_all.at[pl.ds(0, NX - 1)], rep_sem.at[1])
    fill(cur_all.at[pl.ds(0, NX - 1)], rep_sem.at[3])
    for p in range(PARTS):
        rows = pl.ds(p * BLOCK, BLOCK)
        row = p * BLOCK + lax.broadcasted_iota(jnp.int32, (BLOCK, BATCH), 0)
        for r in range(NX):
            refresh[rows, pl.ds(r * BATCH, BATCH)] = (br_all[r] == row).astype(F32).astype(BF16)
    new_rows = jnp.concatenate([cur_all[...].reshape(NX * BATCH, H), jnp.ones((NX * BATCH, H), BF16)], 1)
    for p in range(PARTS):
        rows = pl.ds(p * BLOCK, BLOCK)
        put = dot(refresh[rows, :], new_rows)
        kept = put[:, H:] == 0.0
        new_in[rows, :] = jnp.where(kept, hist[rows, pl.ds(0, H)].astype(F32), put[:, :H]).astype(BF16)
        base_mid[rows, :] = jnp.where(kept, hist[rows, pl.ds(H, H)].astype(F32), 0.0).astype(BF16)
    for c in copies[8:]:
        c.wait()

    for wave in range(WAVES):
        pairs = [pair for pair in ORDER if WAVE[pair] == wave]
        fill(halo.at[pl.ds(0, len(pairs) * CORES - (1 if (NZ - 1, 0) in pairs else 0))], h_recv.at[wave])
        for j, ky in pairs:
            yy, zz = (y + NY - ky) % NY, (z + NZ - FAR[j]) % NZ
            block = halo[pl.ds((j * NY + yy) * CORES, CORES)].astype(F32)
            both = [block[:, :CAP, :].reshape(CORES * CAP, H), block[:, CAP:, :].reshape(CORES * CAP, H)]
            rows = pl.ds(pl.multiple_of(zz * CORES * CAP, CORES * CAP), CORES * CAP)
            tiles[RB + yy, rows, :] = jnp.concatenate(both, 1).astype(BF16)

    sums = []
    for r in range(RB):
        left = jnp.concatenate([adj_v[r, k] for k in range(NB)], 1)
        right = jnp.concatenate([tiles[cols[r, k]] for k in range(NB)], 0)
        sums.append(dot(left, right))
    agg = jnp.concatenate(sums, 0)
    init = ALPHA * init_v[...].astype(F32)
    support_a = ((1.0 - ALPHA) * agg[:, :H] + init).astype(BF16)
    preact_a = (1.0 - BETA_A) * support_a.astype(F32) + BETA_A * dot(support_a, wa_v[...])
    fresh = jnp.maximum(preact_a, 0.0).astype(BF16)
    fresh_all[x] = fresh
    agg_b = agg[:, H:] + dot(f_fwd[...], jnp.concatenate([fresh, fresh], 0))
    support_b = ((1.0 - ALPHA) * agg_b + init).astype(BF16)
    preact_b = (1.0 - BETA_B) * support_b.astype(F32) + BETA_B * dot(support_b, wb_v[...])
    final_out[...] = jnp.maximum(preact_b, 0.0).astype(BF16)
    gated_b = jnp.where(preact_b > 0, up_v[...].astype(F32), 0.0).astype(BF16)
    part[pl.ds(H, H), :] = (BETA_B * dot_t(support_b, gated_b)).astype(BF16)
    back = lax.dot_general(gated_b, wb_v[...], (((1,), (1,)), ((), ())), preferred_element_type=F32)
    support_grad = (1.0 - BETA_B) * gated_b.astype(F32) + BETA_B * back
    agg_grad = ((1.0 - ALPHA) * support_grad).astype(BF16)
    fresh_grad = dot(f_bwd[...], jnp.concatenate([agg_grad, agg_grad], 0))
    gated_a = jnp.where(preact_a > 0, fresh_grad, 0.0).astype(BF16)
    part[pl.ds(0, H), :] = (BETA_A * dot_t(support_a, gated_a)).astype(BF16)

    group = x * CORES + core
    friends = []
    for k in X_ORDER + (0,):
        for other in range(CORES):
            if k or other:
                to_x, to_core = (x + k) % NX, (core + other) % CORES
                friends.append((to_x * CORES + to_core, dev(y, z * CORES + to_core, to_x)))
    for to, device in friends:
        rows = pl.ds(pl.multiple_of(to * PIECE, PIECE), PIECE)
        send(part.at[rows, :], sum_g.at[group], red_sem.at[0], red_sem.at[1], device)
    sum_g[group] = part[pl.ds(pl.multiple_of(group * PIECE, PIECE), PIECE), :]
    fill(sum_g.at[pl.ds(0, GROUP - 1)], red_sem.at[1])
    sum_z[z] = jnp.sum(sum_g[...].astype(F32), 0).astype(BF16)
    for k in FAR[:-1]:
        to = (z + k) % NZ * CORES + core
        send(sum_z.at[z], sum_z.at[z], red_sem.at[2], red_sem.at[3], dev(y, to, x))
    fill(sum_z.at[pl.ds(0, NZ - 1)], red_sem.at[3])
    sum_y[y] = jnp.sum(sum_z[...].astype(F32), 0).astype(BF16)
    for k in FAR[:-1]:
        send(sum_y.at[y], sum_y.at[y], red_sem.at[4], red_sem.at[5], dev((y + k) % NY, w, x))
    for k in X_ORDER:
        send(fresh_all.at[x], fresh_all.at[x], rep_sem.at[4], rep_sem.at[5], dev(y, w, (x + k) % NX))
    fill(sum_y.at[pl.ds(0, NY - 1)], red_sem.at[5])
    total[group] = (jnp.sum(sum_y[...].astype(F32), 0) * SCALE).astype(BF16)
    for _, device in friends:
        send(total.at[group], total.at[group], red_sem.at[6], red_sem.at[7], device)

    fill(fresh_all.at[pl.ds(0, NX - 1)], rep_sem.at[5])
    fresh_rows = fresh_all[...].reshape(NX * BATCH, H)
    for p in range(PARTS):
        rows = pl.ds(p * BLOCK, BLOCK)
        put = dot(refresh[rows, :], fresh_rows)
        new_mid[rows, :] = (put + base_mid[rows, :].astype(F32)).astype(BF16)

    fill(total.at[pl.ds(0, GROUP - 1)], red_sem.at[7])
    half = GROUP // 2
    grad_a[...] = total[pl.ds(0, half)].astype(F32).reshape(H, H)
    grad_b[...] = total[pl.ds(half, half)].astype(F32).reshape(H, H)

    fill(asked_y.at[pl.ds(0, NY - 1)], y_sem.at[0])
    fill(asked_w.at[pl.ds(0, NW - 1)], w_sem.at[0])
    fill(br_all.at[pl.ds(0, NX - 1)], rep_sem.at[0])
    fill(cur_all.at[pl.ds(0, NX - 1)], rep_sem.at[2])
    fill(fresh_all.at[pl.ds(0, NX - 1)], rep_sem.at[4])
    fill(halo.at[pl.ds(0, NY * NW - 1)], h_send)
    fill(sum_g.at[pl.ds(0, GROUP - 1)], red_sem.at[0])
    fill(sum_z.at[pl.ds(0, NZ - 1)], red_sem.at[2])
    fill(sum_y.at[pl.ds(0, NY - 1)], red_sem.at[4])
    fill(total.at[pl.ds(0, GROUP - 1)], red_sem.at[6])


def write_out(*refs):
    sems = refs[-1]
    copies = [pltpu.make_async_copy(refs[i], refs[5 + i], sems.at[i]) for i in range(5)]
    for c in copies:
        c.start()
    for c in copies:
        c.wait()


def on_device(
    history_in,
    history_mid,
    current,
    initial,
    batch_rows,
    halo_rows,
    halo_count,
    adj_cols,
    adj_vals,
    upstream,
    weight_a,
    weight_b,
):
    vmem = pl.BlockSpec(memory_space=pltpu.VMEM)
    hbm = pl.BlockSpec(memory_space=pltpu.HBM)
    sds = jax.ShapeDtypeStruct
    dma = pltpu.SemaphoreType.DMA
    results = pl.pallas_call(
        kernel,
        name="gcn",
        out_shape=(
            sds((BATCH, H), BF16),
            sds((SHARD, H), BF16),
            sds((SHARD, H), BF16),
            sds((H, H), F32),
            sds((H, H), F32),
        ),
        in_specs=[hbm] * 12,
        out_specs=(vmem,) * 5,
        scratch_shapes=[
            pltpu.VMEM((CAP, NY * NW), jnp.int32),
            pltpu.VMEM((1, NY * NW), jnp.int32),
            pltpu.SMEM((RB, NB), jnp.int32),
            pltpu.VMEM((NY, CAP, NY * NW), jnp.int32),
            pltpu.VMEM((128, 128), jnp.int32),
            pltpu.VMEM((NW, 1, 128), jnp.int32),
            pltpu.VMEM((NW, 1, 128), jnp.int32),
            pltpu.VMEM((SHARD, 2 * H), BF16),
            pltpu.VMEM((ROWS, SHARD), BF16),
            pltpu.VMEM((NW, NY, 2 * CAP, H), BF16),
            pltpu.VMEM((NY * NW, 2 * CAP, H), BF16),
            pltpu.VMEM((RB + NY, TILE, 2 * H), BF16),
            pltpu.VMEM((RB, NB, TILE, TILE), BF16),
            pltpu.VMEM((NX, BATCH, H), BF16),
            pltpu.VMEM((NX, BATCH, H), BF16),
            pltpu.VMEM((NX, 1, BATCH), jnp.int32),
            pltpu.VMEM((SHARD, NX * BATCH), BF16),
            pltpu.VMEM((SHARD, H), BF16),
            pltpu.VMEM((BATCH, H), BF16),
            pltpu.VMEM((BATCH, H), BF16),
            pltpu.VMEM((H, H), BF16),
            pltpu.VMEM((H, H), BF16),
            pltpu.VMEM((BATCH, 2 * BATCH), BF16),
            pltpu.VMEM((BATCH, 2 * BATCH), BF16),
            pltpu.VMEM((2 * H, H), BF16),
            pltpu.VMEM((GROUP, PIECE, H), BF16),
            pltpu.VMEM((NZ, PIECE, H), BF16),
            pltpu.VMEM((NY, PIECE, H), BF16),
            pltpu.VMEM((GROUP, PIECE, H), BF16),
            dma((12,)),
            dma((2,)),
            dma((2,)),
            dma,
            dma((WAVES,)),
            dma((6,)),
            dma((8,)),
        ],
        compiler_params=pltpu.CompilerParams(
            collective_id=0, has_side_effects=True, vmem_limit_bytes=VMEM
        ),
    )(*[pltpu.with_memory_space_constraint(a, pltpu.HBM) for a in (
        halo_rows[0].T,
        halo_count,
        batch_rows[None, :],
        adj_cols[0],
        history_in,
        history_mid,
        current,
        initial,
        upstream,
        adj_vals[0],
        weight_a,
        weight_b,
    )])
    return pl.pallas_call(
        write_out,
        name="write_out",
        out_shape=tuple(sds(r.shape, r.dtype) for r in results),
        in_specs=[vmem] * 5,
        out_specs=(hbm,) * 5,
        scratch_shapes=[dma((5,))],
        compiler_params=pltpu.CompilerParams(vmem_limit_bytes=4 * 2**20),
    )(*results)


def solution(mesh):
    both = ("node", "rep")
    in_specs = (
        P("node", None),
        P("node", None),
        P(both, None),
        P(both, None),
        P(both),
        P(both, None, None),
        P(both, None),
        P(both, None, None),
        P(both, None, None, None, None),
        P(both, None),
        P(),
        P(),
    )
    out_specs = (P(both, None), P("node", None), P("node", None), P(), P())
    return jax.shard_map(on_device, mesh=mesh, in_specs=in_specs, out_specs=out_specs, check_vma=False)
```

```python
import math

import jax
import jax.numpy as jnp
from jax import lax
from jax.experimental import pallas as pl
from jax.experimental.pallas import tpu as pltpu
from jax.sharding import PartitionSpec as P

ALPHA = 0.1
BETA_A = math.log(1.0 + 0.5 / 3.0)
BETA_B = math.log(1.0 + 0.5 / 4.0)
MESH = pl.DeviceIdType.MESH
F32 = jnp.float32
BF16 = jnp.bfloat16

NY = 8
NW = 16
NX = 4
CAP = 8
TILE = 128
H = 128
BATCH = 256
SHARD = 2048
RB = 2
NB = 8
NZ = 8
CORES = 2
FAR = (4, 3, 5, 2, 6, 1, 7, 0)
W_ORDER = (8, 7, 9, 6, 10, 5, 11, 4, 12, 3, 13, 2, 14, 1, 15)
X_ORDER = (2, 1, 3)
CHUNKS = ((0,), (1,), (2, 3), (4, 5), (6, 7))
ROWS = NY * CAP * CORES * 2
WAVES = 4
GROUP = NX * CORES
PIECE = 2 * H // GROUP
SCALE = 1.0 / math.sqrt(NY * NW * NX * BATCH)


def hops(pair):
    j, ky = pair
    dz, dy = min(FAR[j], NZ - FAR[j]), min(ky, NY - ky)
    return -max(dz, dy), -dz - dy


def schedule():
    steps, left = [], []
    for chunk, some in zip(CHUNKS, (8, 0, 0, 0, 64)):
        left = sorted(left + [(j, ky) for j in chunk for ky in FAR], key=hops)
        steps.append(left[:some])
        left = left[some:]
    return steps


STEPS = schedule()
ORDER = [pair for step in STEPS for pair in step]
WAVE = {pair: i * WAVES // len(ORDER) for i, pair in enumerate(ORDER)}
PARTS = 8
BLOCK = SHARD // PARTS
VMEM = 40 * 2**20


def fill(ref, sem):
    pltpu.make_async_copy(ref, ref, sem).wait()


def dot(lhs, rhs):
    return jnp.dot(lhs, rhs, preferred_element_type=F32)


def dot_t(lhs, rhs):
    return lax.dot_general(lhs, rhs, (((0,), (0,)), ((), ())), preferred_element_type=F32)


def kernel(
    halo_rows,
    halo_count,
    batch_rows,
    adj_cols,
    hist_in,
    hist_mid,
    current,
    initial,
    upstream,
    adj,
    weight_a,
    weight_b,
    final_out,
    new_in,
    new_mid,
    grad_a,
    grad_b,
    list_v,
    count_v,
    cols,
    asked_y,
    asked_t,
    ask_row,
    asked_w,
    hist,
    onehot,
    rows_out,
    halo,
    tiles,
    adj_v,
    cur_all,
    fresh_all,
    br_all,
    refresh,
    base_mid,
    init_v,
    up_v,
    wa_v,
    wb_v,
    f_fwd,
    f_bwd,
    part,
    sum_g,
    sum_z,
    sum_y,
    total,
    load_sem,
    y_sem,
    w_sem,
    h_send,
    h_recv,
    rep_sem,
    red_sem,
):
    node, x = lax.axis_index("node"), lax.axis_index("rep")
    y, w = node // NW, node % NW
    z, core = w // CORES, w % CORES

    def dev(yy, ww, xx):
        return (yy * NW + ww, xx)

    def send(src, dst, s_sem, r_sem, device):
        pltpu.make_async_remote_copy(
            src_ref=src, dst_ref=dst, send_sem=s_sem, recv_sem=r_sem, device_id=device, device_id_type=MESH
        ).start()

    loads = [
        (halo_rows, list_v),
        (halo_count, count_v),
        (batch_rows, br_all.at[x]),
        (adj_cols, cols),
        (hist_in, hist.at[:, pl.ds(0, H)]),
        (hist_mid, hist.at[:, pl.ds(H, H)]),
        (current, cur_all.at[x]),
        (adj, adj_v),
        (initial, init_v),
        (upstream, up_v),
        (weight_a, wa_v),
        (weight_b, wb_v),
    ]
    copies = [pltpu.make_async_copy(s, d, load_sem.at[i]) for i, (s, d) in enumerate(loads)]
    copies[0].start()
    copies[1].start()

    barrier = pltpu.get_barrier_semaphore()
    for k in FAR[:-1]:
        pl.semaphore_signal(barrier, inc=1, device_id=dev((y + k) % NY, w, x), device_id_type=MESH)
    for k in W_ORDER:
        pl.semaphore_signal(barrier, inc=1, device_id=dev(y, (w + k) % NW, x), device_id_type=MESH)
    for k in range(1, NX):
        pl.semaphore_signal(barrier, inc=1, device_id=dev(y, w, (x + k) % NX), device_id_type=MESH)

    slot = lax.broadcasted_iota(jnp.int32, (CAP, NY * NW), 0)
    copies[0].wait()
    copies[1].wait()
    asked_y[y] = jnp.where(slot < count_v[...], list_v[...], -1)
    pl.semaphore_wait(barrier, NY + NW + NX - 3)

    for k in FAR[:-1]:
        send(asked_y.at[y], asked_y.at[y], y_sem.at[0], y_sem.at[1], dev((y + k) % NY, w, x))
    for c in copies[2:]:
        c.start()
    copies[2].wait()
    copies[6].wait()
    for k in X_ORDER:
        to = dev(y, w, (x + k) % NX)
        send(br_all.at[x], br_all.at[x], rep_sem.at[0], rep_sem.at[1], to)
        send(cur_all.at[x], cur_all.at[x], rep_sem.at[2], rep_sem.at[3], to)

    fill(asked_y.at[pl.ds(0, NY - 1)], y_sem.at[1])
    lists = asked_y[...].reshape(NY * CAP, NY * NW)
    lists = jnp.concatenate([lists, jnp.zeros((128 - NY * CAP, NY * NW), jnp.int32)], 0)
    asked_t[...] = lists.T
    mine = asked_t[pl.ds(pl.multiple_of(y * NW, NW), NW), :]
    for i in range(NW):
        ask_row[i] = mine[i : i + 1, :]
    for j, k in enumerate(FAR):
        for other in range(CORES):
            if k or other:
                to = (z + NZ - k) % NZ * CORES + (core + other) % CORES
                send(ask_row.at[to], asked_w.at[CORES * j + core], w_sem.at[0], w_sem.at[1], dev(y, to, x))
    asked_w[NW - CORES + core] = ask_row[w]

    fill(asked_w.at[pl.ds(0, NW - 1)], w_sem.at[1])
    wanted = jnp.concatenate([asked_w[i] for i in range(NW)] + [jnp.zeros((128 - NW, 128), jnp.int32)], 0)
    asked_t[...] = wanted.T
    wanted = asked_t[pl.ds(0, NY * CAP), :]
    lane = lax.broadcasted_iota(jnp.int32, (NY * CAP, SHARD), 1)
    for c, chunk in enumerate(CHUNKS):
        first, lists = chunk[0] * CORES, len(chunk) * CORES
        for q in range(lists):
            hit = jnp.broadcast_to(wanted[:, first + q : first + q + 1], (NY * CAP, SHARD)) == lane
            onehot[pl.ds(q * NY * CAP, NY * CAP), :] = hit.astype(F32).astype(BF16)
        if c == 0:
            copies[4].wait()
            copies[5].wait()
        got = dot(onehot[pl.ds(0, lists * NY * CAP), :], hist[...])
        both = jnp.concatenate([got[:, :H].reshape(lists * NY, CAP, H), got[:, H:].reshape(lists * NY, CAP, H)], 1)
        rows_out[pl.ds(first, lists)] = both.astype(BF16).reshape(lists, NY, 2 * CAP, H)
        for j, ky in STEPS[c]:
            for other in range(CORES):
                if FAR[j] or ky or other:
                    to_core, to_y = (core + other) % CORES, (y + ky) % NY
                    to_w = (z + FAR[j]) % NZ * CORES + to_core
                    src = rows_out.at[CORES * j + to_core, to_y]
                    dst = halo.at[(j * NY + y) * CORES + core]
                    send(src, dst, h_send, h_recv.at[WAVE[j, ky]], dev(to_y, to_w, x))
    halo[((NZ - 1) * NY + y) * CORES + core] = rows_out[NW - CORES + core, y]

    copies[3].wait()
    copies[7].wait()
    for r in range(RB):
        for c in range(RB):
            acc = jnp.zeros((TILE, TILE), F32)
            for k in range(NB):
                acc = acc + jnp.where(cols[r, k] == c, adj_v[r, k].astype(F32), 0.0)
            high = acc.astype(BF16)
            low = (acc - high.astype(F32)).astype(BF16)
            rs, cs = pl.ds(r * TILE, TILE), pl.ds(c * TILE, TILE)
            f_fwd[rs, cs] = high
            f_fwd[rs, pl.ds(BATCH + c * TILE, TILE)] = low
            acc_t = acc.T
            high_t = acc_t.astype(BF16)
            f_bwd[cs, rs] = high_t
            f_bwd[cs, pl.ds(BATCH + r * TILE, TILE)] = (acc_t - high_t.astype(F32)).astype(BF16)
    for c in range(RB):
        tiles[c, :, pl.ds(0, H)] = cur_all[x, pl.ds(c * TILE, TILE), :]
        tiles[c, :, pl.ds(H, H)] = jnp.zeros((TILE, H), BF16)

    fill(br_all.at[pl.ds(0, NX - 1)], rep_sem.at[1])
    fill(cur_all.at[pl.ds(0, NX - 1)], rep_sem.at[3])
    for p in range(PARTS):
        rows = pl.ds(p * BLOCK, BLOCK)
        row = p * BLOCK + lax.broadcasted_iota(jnp.int32, (BLOCK, BATCH), 0)
        for r in range(NX):
            refresh[rows, pl.ds(r * BATCH, BATCH)] = (br_all[r] == row).astype(F32).astype(BF16)
    new_rows = jnp.concatenate([cur_all[...].reshape(NX * BATCH, H), jnp.ones((NX * BATCH, H), BF16)], 1)
    for p in range(PARTS):
        rows = pl.ds(p * BLOCK, BLOCK)
        put = dot(refresh[rows, :], new_rows)
        kept = put[:, H:] == 0.0
        new_in[rows, :] = jnp.where(kept, hist[rows, pl.ds(0, H)].astype(F32), put[:, :H]).astype(BF16)
        base_mid[rows, :] = jnp.where(kept, hist[rows, pl.ds(H, H)].astype(F32), 0.0).astype(BF16)
    for c in copies[8:]:
        c.wait()

    for wave in range(WAVES):
        pairs = [pair for pair in ORDER if WAVE[pair] == wave]
        fill(halo.at[pl.ds(0, len(pairs) * CORES - (1 if (NZ - 1, 0) in pairs else 0))], h_recv.at[wave])
        for j, ky in pairs:
            yy, zz = (y + NY - ky) % NY, (z + NZ - FAR[j]) % NZ
            block = halo[pl.ds((j * NY + yy) * CORES, CORES)].astype(F32)
            both = [block[:, :CAP, :].reshape(CORES * CAP, H), block[:, CAP:, :].reshape(CORES * CAP, H)]
            rows = pl.ds(pl.multiple_of(zz * CORES * CAP, CORES * CAP), CORES * CAP)
            tiles[RB + yy, rows, :] = jnp.concatenate(both, 1).astype(BF16)

    sums = []
    for r in range(RB):
        left = jnp.concatenate([adj_v[r, k] for k in range(NB)], 1)
        right = jnp.concatenate([tiles[cols[r, k]] for k in range(NB)], 0)
        sums.append(dot(left, right))
    agg = jnp.concatenate(sums, 0)
    init = ALPHA * init_v[...].astype(F32)
    support_a = ((1.0 - ALPHA) * agg[:, :H] + init).astype(BF16)
    preact_a = (1.0 - BETA_A) * support_a.astype(F32) + BETA_A * dot(support_a, wa_v[...])
    fresh = jnp.maximum(preact_a, 0.0).astype(BF16)
    fresh_all[x] = fresh
    agg_b = agg[:, H:] + dot(f_fwd[...], jnp.concatenate([fresh, fresh], 0))
    support_b = ((1.0 - ALPHA) * agg_b + init).astype(BF16)
    preact_b = (1.0 - BETA_B) * support_b.astype(F32) + BETA_B * dot(support_b, wb_v[...])
    final_out[...] = jnp.maximum(preact_b, 0.0).astype(BF16)
    gated_b = jnp.where(preact_b > 0, up_v[...].astype(F32), 0.0).astype(BF16)
    part[pl.ds(H, H), :] = (BETA_B * dot_t(support_b, gated_b)).astype(BF16)
    back = lax.dot_general(gated_b, wb_v[...], (((1,), (1,)), ((), ())), preferred_element_type=F32)
    support_grad = (1.0 - BETA_B) * gated_b.astype(F32) + BETA_B * back
    agg_grad = ((1.0 - ALPHA) * support_grad).astype(BF16)
    fresh_grad = dot(f_bwd[...], jnp.concatenate([agg_grad, agg_grad], 0))
    gated_a = jnp.where(preact_a > 0, fresh_grad, 0.0).astype(BF16)
    part[pl.ds(0, H), :] = (BETA_A * dot_t(support_a, gated_a)).astype(BF16)

    group = x * CORES + core
    friends = []
    for k in X_ORDER + (0,):
        for other in range(CORES):
            if k or other:
                to_x, to_core = (x + k) % NX, (core + other) % CORES
                friends.append((to_x * CORES + to_core, dev(y, z * CORES + to_core, to_x)))
    for to, device in friends:
        rows = pl.ds(pl.multiple_of(to * PIECE, PIECE), PIECE)
        send(part.at[rows, :], sum_g.at[group], red_sem.at[0], red_sem.at[1], device)
    sum_g[group] = part[pl.ds(pl.multiple_of(group * PIECE, PIECE), PIECE), :]
    fill(sum_g.at[pl.ds(0, GROUP - 1)], red_sem.at[1])
    sum_z[z] = jnp.sum(sum_g[...].astype(F32), 0).astype(BF16)
    for k in FAR[:-1]:
        to = (z + k) % NZ * CORES + core
        send(sum_z.at[z], sum_z.at[z], red_sem.at[2], red_sem.at[3], dev(y, to, x))
    fill(sum_z.at[pl.ds(0, NZ - 1)], red_sem.at[3])
    sum_y[y] = jnp.sum(sum_z[...].astype(F32), 0).astype(BF16)
    for k in FAR[:-1]:
        send(sum_y.at[y], sum_y.at[y], red_sem.at[4], red_sem.at[5], dev((y + k) % NY, w, x))
    for k in X_ORDER:
        send(fresh_all.at[x], fresh_all.at[x], rep_sem.at[4], rep_sem.at[5], dev(y, w, (x + k) % NX))
    fill(sum_y.at[pl.ds(0, NY - 1)], red_sem.at[5])
    total[group] = (jnp.sum(sum_y[...].astype(F32), 0) * SCALE).astype(BF16)
    for _, device in friends:
        send(total.at[group], total.at[group], red_sem.at[6], red_sem.at[7], device)

    fill(fresh_all.at[pl.ds(0, NX - 1)], rep_sem.at[5])
    fresh_rows = fresh_all[...].reshape(NX * BATCH, H)
    for p in range(PARTS):
        rows = pl.ds(p * BLOCK, BLOCK)
        put = dot(refresh[rows, :], fresh_rows)
        new_mid[rows, :] = (put + base_mid[rows, :].astype(F32)).astype(BF16)

    fill(total.at[pl.ds(0, GROUP - 1)], red_sem.at[7])
    half = GROUP // 2
    grad_a[...] = total[pl.ds(0, half)].astype(F32).reshape(H, H)
    grad_b[...] = total[pl.ds(half, half)].astype(F32).reshape(H, H)

    fill(asked_y.at[pl.ds(0, NY - 1)], y_sem.at[0])
    fill(asked_w.at[pl.ds(0, NW - 1)], w_sem.at[0])
    fill(br_all.at[pl.ds(0, NX - 1)], rep_sem.at[0])
    fill(cur_all.at[pl.ds(0, NX - 1)], rep_sem.at[2])
    fill(fresh_all.at[pl.ds(0, NX - 1)], rep_sem.at[4])
    fill(halo.at[pl.ds(0, NY * NW - 1)], h_send)
    fill(sum_g.at[pl.ds(0, GROUP - 1)], red_sem.at[0])
    fill(sum_z.at[pl.ds(0, NZ - 1)], red_sem.at[2])
    fill(sum_y.at[pl.ds(0, NY - 1)], red_sem.at[4])
    fill(total.at[pl.ds(0, GROUP - 1)], red_sem.at[6])


def write_out(*refs):
    sems = refs[-1]
    copies = [pltpu.make_async_copy(refs[i], refs[5 + i], sems.at[i]) for i in range(5)]
    for c in copies:
        c.start()
    for c in copies:
        c.wait()


def on_device(
    history_in,
    history_mid,
    current,
    initial,
    batch_rows,
    halo_rows,
    halo_count,
    adj_cols,
    adj_vals,
    upstream,
    weight_a,
    weight_b,
):
    vmem = pl.BlockSpec(memory_space=pltpu.VMEM)
    hbm = pl.BlockSpec(memory_space=pltpu.HBM)
    sds = jax.ShapeDtypeStruct
    dma = pltpu.SemaphoreType.DMA
    results = pl.pallas_call(
        kernel,
        name="gcn",
        out_shape=(
            sds((BATCH, H), BF16),
            sds((SHARD, H), BF16),
            sds((SHARD, H), BF16),
            sds((H, H), F32),
            sds((H, H), F32),
        ),
        in_specs=[hbm] * 12,
        out_specs=(vmem,) * 5,
        scratch_shapes=[
            pltpu.VMEM((CAP, NY * NW), jnp.int32),
            pltpu.VMEM((1, NY * NW), jnp.int32),
            pltpu.SMEM((RB, NB), jnp.int32),
            pltpu.VMEM((NY, CAP, NY * NW), jnp.int32),
            pltpu.VMEM((128, 128), jnp.int32),
            pltpu.VMEM((NW, 1, 128), jnp.int32),
            pltpu.VMEM((NW, 1, 128), jnp.int32),
            pltpu.VMEM((SHARD, 2 * H), BF16),
            pltpu.VMEM((ROWS, SHARD), BF16),
            pltpu.VMEM((NW, NY, 2 * CAP, H), BF16),
            pltpu.VMEM((NY * NW, 2 * CAP, H), BF16),
            pltpu.VMEM((RB + NY, TILE, 2 * H), BF16),
            pltpu.VMEM((RB, NB, TILE, TILE), BF16),
            pltpu.VMEM((NX, BATCH, H), BF16),
            pltpu.VMEM((NX, BATCH, H), BF16),
            pltpu.VMEM((NX, 1, BATCH), jnp.int32),
            pltpu.VMEM((SHARD, NX * BATCH), BF16),
            pltpu.VMEM((SHARD, H), BF16),
            pltpu.VMEM((BATCH, H), BF16),
            pltpu.VMEM((BATCH, H), BF16),
            pltpu.VMEM((H, H), BF16),
            pltpu.VMEM((H, H), BF16),
            pltpu.VMEM((BATCH, 2 * BATCH), BF16),
            pltpu.VMEM((BATCH, 2 * BATCH), BF16),
            pltpu.VMEM((2 * H, H), BF16),
            pltpu.VMEM((GROUP, PIECE, H), BF16),
            pltpu.VMEM((NZ, PIECE, H), BF16),
            pltpu.VMEM((NY, PIECE, H), BF16),
            pltpu.VMEM((GROUP, PIECE, H), BF16),
            dma((12,)),
            dma((2,)),
            dma((2,)),
            dma,
            dma((WAVES,)),
            dma((6,)),
            dma((8,)),
        ],
        compiler_params=pltpu.CompilerParams(
            collective_id=0, has_side_effects=True, vmem_limit_bytes=VMEM
        ),
    )(*[pltpu.with_memory_space_constraint(a, pltpu.HBM) for a in (
        halo_rows[0].T,
        halo_count,
        batch_rows[None, :],
        adj_cols[0],
        history_in,
        history_mid,
        current,
        initial,
        upstream,
        adj_vals[0],
        weight_a,
        weight_b,
    )])
    return pl.pallas_call(
        write_out,
        name="write_out",
        out_shape=tuple(sds(r.shape, r.dtype) for r in results),
        in_specs=[vmem] * 5,
        out_specs=(hbm,) * 5,
        scratch_shapes=[dma((5,))],
        compiler_params=pltpu.CompilerParams(vmem_limit_bytes=4 * 2**20),
    )(*results)


def solution(mesh):
    both = ("node", "rep")
    in_specs = (
        P("node", None),
        P("node", None),
        P(both, None),
        P(both, None),
        P(both),
        P(both, None, None),
        P(both, None),
        P(both, None, None),
        P(both, None, None, None, None),
        P(both, None),
        P(),
        P(),
    )
    out_specs = (P(both, None), P("node", None), P("node", None), P(), P())
    return jax.shard_map(on_device, mesh=mesh, in_specs=in_specs, out_specs=out_specs, check_vma=False)
```
